32 devices in a mesh: groups: 2 (over y), wide: 8 (over z, core), narrow: 2 (over x).
Axes of the slice: x: 2, y: 2, z: 4, core: 2. Of those that a mesh axis runs over, the one named last changes fastest.
Arguments:
- tokens: bfloat16 [192, 16384], P(('groups', 'narrow'), 'wide'), parts along dimension 0, may hold values from -64 to 64
- norm_gain: bfloat16 [16384], P('wide'), may hold values from 0.099609375 to 1.8984375
- w_query: bfloat16 [16384, 16384], P('wide', 'narrow'), may hold values from -0.046875 to 0.046875
- w_key: bfloat16 [16384, 1024], P('wide', 'narrow'), may hold values from -0.046875 to 0.046875
- w_value: bfloat16 [16384, 1024], P('wide', 'narrow'), may hold values from -0.046875 to 0.046875
- w_out: bfloat16 [16384, 16384], P('narrow', 'wide'), may hold values from -0.046875 to 0.046875
- cache_key: bfloat16 [192, 256, 1024], P(('groups', 'wide'), None, 'narrow'), parts along dimension 0, may hold values from -400 to 400
- cache_value: bfloat16 [192, 256, 1024], P(('groups', 'wide'), None, 'narrow'), parts along dimension 0, may hold values from -24 to 24
- lengths: int32 [192], P('groups'), parts along dimension 0, may hold values from 2 to 256, as said below
Outputs:
- attended: bfloat16 [192, 16384], P(('groups', 'narrow'), 'wide'), parts along dimension 0
The draws below stay inside these ranges and needn't reach their ends.
There are 2 independent parts, one for each index of `groups`. The reference program is written for one: setup_inputs(seed, part) draws one part's arguments, and reference() takes and returns one part's arrays. A program takes and returns all parts, laid end to end along the dimension named above; an argument that names none is the same for every part. Nothing has to cross between parts.
Inputs may be any that keep to these rules, and one draw needn't show every extreme that they name: `lengths`: each row has at least two filled slots, and some row fills all 256 slots.
All inputs are finite; a program needn't handle non-finite values.
Results may differ from the reference program's by a relative error of at most 0.012.
The reference program's roundings to bfloat16 on the way count: a program that leaves them out, or rounds other values in their place, can miss the bound.
Values may be sent and summed in bfloat16 or wider, within the bound.
A program may use at most 192 MiB of HBM per device.

```python
import math
import jax
import jax.numpy as jnp
from jax import lax

D = 16384
HQ = 128
KVH = 8
HD = 128
CACHE_LEN = 256
ROWS = 96
N_NARROW = 2


def draw_tokens(key, part):
    key = jax.random.fold_in(key, 5)
    key_one = jax.random.fold_in(key, 0)
    position_ramp = jnp.arange(D, dtype=jnp.float32) / D
    entries = jnp.clip(jax.random.normal(key_one, (ROWS, D), jnp.float32), -6.0, 6.0) * jnp.exp(position_ramp * math.log(3.0))[None, :]
    return entries.astype(jnp.bfloat16)


def draw_cache_key(key, part):
    key = jax.random.fold_in(key, 11)
    key_one = jax.random.fold_in(key, 0)
    array_shape = (ROWS, CACHE_LEN, KVH * HD)
    entries = jnp.clip(jax.random.normal(key_one, array_shape, jnp.float32), -6.0, 6.0)
    return entries.astype(jnp.bfloat16)


def draw_lengths(key, part):
    key = jax.random.fold_in(key, 7)
    key_one, key_two, key_three = jax.random.split(key, 3)
    top_power = CACHE_LEN.bit_length() - 1
    exponent = jax.random.randint(key_one, (ROWS,), 1, top_power)
    lowest = jnp.left_shift(jnp.ones((ROWS,), jnp.int32), exponent)
    length = lowest + jax.random.randint(key_two, (ROWS,), 0, lowest)
    longest = jax.random.randint(key_three, (), 0, ROWS)
    return jnp.where(jnp.arange(ROWS) == longest, CACHE_LEN, length).astype(jnp.int32)


def shard_levels(own_key, extent, cuts, low, top_value):
    gain = 1.0
    for position, blocks in cuts:
        draws = jax.random.uniform(jax.random.fold_in(jax.random.fold_in(own_key, 6), position), (blocks,), jnp.float32, low / len(cuts), top_value / len(cuts))
        gain = gain * jnp.repeat(jnp.exp(draws), extent[position] // blocks).reshape((-1,) + (1,) * (len(extent) - 1 - position))
    return gain


def noise(stream_key, extent, width, reach, cuts=(), held_as=jnp.bfloat16):
    loudness = shard_levels(stream_key, extent, cuts, -0.22, 0.18) if cuts else 1.0
    drawn = jax.random.normal(stream_key, extent, jnp.float32) * width * loudness
    return jnp.minimum(jnp.maximum(drawn, -reach), reach).astype(held_as)


def setup_inputs(seed: int = 0, part: int = 0) -> dict:
    key_of = jax.random.split(jax.random.key(seed), 10)
    part_splits = jax.random.split(jax.random.fold_in(key_of[9], part), 10)
    tokens = draw_tokens(jax.random.fold_in(jax.random.fold_in(key_of[9], part), 71), part)
    norm_gain = jnp.clip(1.0 + 0.18 * jax.random.normal(key_of[1], (D,), jnp.float32), 0.099609375, 1.8984375).astype(jnp.bfloat16)
    w_query = noise(key_of[2], (D, HQ * HD), D ** -0.5, 0.046875, ((0, 8), (1, 2)))
    w_key = noise(key_of[3], (D, KVH * HD), D ** -0.5, 0.046875, ((0, 8), (1, 2)))
    w_value = noise(key_of[4], (D, KVH * HD), D ** -0.5, 0.046875, ((0, 8), (1, 2)))
    w_out = noise(key_of[5], (HQ * HD, D), (HQ * HD) ** -0.5, 0.046875, ((0, 2), (1, 8)))
    cache_key = draw_cache_key(jax.random.fold_in(jax.random.fold_in(key_of[9], part), 71), part)
    cache_value = noise(part_splits[7], (ROWS, CACHE_LEN, KVH * HD), 4.0, 24.0, ((0, 8), (2, 2)))
    lengths = draw_lengths(jax.random.fold_in(jax.random.fold_in(key_of[9], part), 71), part)
    return dict(tokens=tokens, norm_gain=norm_gain, w_query=w_query, w_key=w_key, w_value=w_value, w_out=w_out, cache_key=cache_key, cache_value=cache_value, lengths=lengths)


rope_base = 500000.0
norm_eps = 1e-05

def rotate(vectors, positions):
    half_dim = vectors.shape[-1] // 2
    frequency = rope_base ** (-jnp.arange(half_dim, dtype=jnp.float32) / half_dim)
    angles = positions.astype(jnp.float32)[:, None] * frequency[None, :]
    cosine = jnp.cos(angles)[:, None, :]
    sines = jnp.sin(angles)[:, None, :]
    leading_half = vectors[..., :half_dim]
    trailing_half = vectors[..., half_dim:]
    return jnp.concatenate([leading_half * cosine - trailing_half * sines, trailing_half * cosine + leading_half * sines], axis=-1)

def attend(queries, key_new, value_new, cache_key, cache_value, lengths):
    batch_rows, head_count, head_dim = queries.shape
    group_count = key_new.shape[1]
    per_group = head_count // group_count
    token_count = cache_key.shape[1]
    grouped = queries.astype(jnp.float32).reshape(batch_rows, group_count, per_group, head_dim)
    cached_keys = cache_key.astype(jnp.float32).reshape(batch_rows, token_count, group_count, head_dim)
    cached_values = cache_value.astype(jnp.float32).reshape(batch_rows, token_count, group_count, head_dim)
    score_scale = head_dim ** (-0.5)
    scores = jnp.einsum('rgqd,rtgd->rgqt', grouped, cached_keys) * score_scale
    own_score = jnp.einsum('rgqd,rgd->rgq', grouped, key_new.astype(jnp.float32)) * score_scale
    usable = (jnp.arange(token_count)[None, :] < lengths[:, None])[:, None, None, :]
    highest = jnp.maximum(lax.optimization_barrier(jnp.max(jnp.where(usable, scores, -1e+30), axis=-1)), own_score)
    weights = jnp.where(usable, jnp.exp(scores - highest[..., None]), 0.0)
    own_weight = jnp.exp(own_score - highest)
    denominator = lax.optimization_barrier(jnp.sum(weights, axis=-1)) + own_weight
    rounded_weights = weights.astype(jnp.bfloat16).astype(jnp.float32)
    blended = jnp.einsum('rgqt,rtgd->rgqd', rounded_weights, cached_values)
    blended = blended + own_weight[..., None] * value_new.astype(jnp.float32)[:, :, None, :]
    return (blended / denominator[..., None]).astype(jnp.bfloat16).reshape(batch_rows, head_count * head_dim)

def reference(tokens, norm_gain, w_query, w_key, w_value, w_out, cache_key, cache_value, lengths):
    features = tokens.astype(jnp.float32)
    inverse = lax.rsqrt(lax.optimization_barrier(jnp.mean(features * features, axis=1)) + norm_eps)
    scaled = (features * norm_gain.astype(jnp.float32)[None, :]).astype(jnp.bfloat16)
    query_raw = jnp.dot(scaled, w_query, preferred_element_type=jnp.float32) * inverse[:, None]
    key_raw = jnp.dot(scaled, w_key, preferred_element_type=jnp.float32) * inverse[:, None]
    value_raw = jnp.dot(scaled, w_value, preferred_element_type=jnp.float32) * inverse[:, None]
    queries = rotate(query_raw.reshape(ROWS, HQ, HD), lengths).astype(jnp.bfloat16)
    key_new = rotate(key_raw.reshape(ROWS, KVH, HD), lengths).astype(jnp.bfloat16)
    value_new = value_raw.reshape(ROWS, KVH, HD).astype(jnp.bfloat16)
    heads_out = attend(queries, key_new, value_new, cache_key, cache_value, lengths)
    head_block = HQ * HD // N_NARROW
    summed = jnp.zeros((ROWS, D), jnp.float32)
    for part_index in range(N_NARROW):
        partial_term = jnp.dot(heads_out[:, part_index * head_block:(part_index + 1) * head_block], w_out[part_index * head_block:(part_index + 1) * head_block, :], preferred_element_type=jnp.float32)
        summed = summed + lax.optimization_barrier(partial_term.astype(jnp.bfloat16)).astype(jnp.float32)
    return summed.astype(jnp.bfloat16)
```

```python
import functools

import jax
import jax.numpy as jnp
from jax import lax
from jax.experimental import pallas as pl
from jax.experimental.pallas import tpu as pltpu
from jax.sharding import PartitionSpec as P

D = 16384
HD = 128
PAD = 16
PARTS = 4
TILE = 256
MESH = pl.DeviceIdType.MESH


rope_base = 500000.0
norm_eps = 1e-05


def rotate(vectors, positions):
    half_dim = vectors.shape[-1] // 2
    frequency = rope_base ** (-jnp.arange(half_dim, dtype=jnp.float32) / half_dim)
    angles = positions.astype(jnp.float32)[:, None] * frequency[None, :]
    cosine = jnp.cos(angles)[:, None, :]
    sines = jnp.sin(angles)[:, None, :]
    leading_half = vectors[..., :half_dim]
    trailing_half = vectors[..., half_dim:]
    return jnp.concatenate(
        [
            leading_half * cosine - trailing_half * sines,
            trailing_half * cosine + leading_half * sines,
        ],
        axis=-1,
    )


def attend(queries, key_new, value_new, cache_key, cache_value, lengths):
    batch_rows, head_count, head_dim = queries.shape
    group_count = key_new.shape[1]
    per_group = head_count // group_count
    token_count = cache_key.shape[1]
    grouped = queries.reshape(batch_rows, group_count, per_group, head_dim)
    cached_keys = cache_key.reshape(batch_rows, token_count, group_count, head_dim)
    cached_values = cache_value.reshape(batch_rows, token_count, group_count, head_dim)
    score_scale = head_dim ** (-0.5)
    scores = (
        jnp.einsum("rgqd,rtgd->rgqt", grouped, cached_keys, preferred_element_type=jnp.float32)
        * score_scale
    )
    own_score = (
        jnp.einsum("rgqd,rgd->rgq", grouped, key_new, preferred_element_type=jnp.float32)
        * score_scale
    )
    usable = (jnp.arange(token_count)[None, :] < lengths[:, None])[:, None, None, :]
    highest = jnp.maximum(jnp.max(jnp.where(usable, scores, -1e30), axis=-1), own_score)
    weights = jnp.where(usable, jnp.exp(scores - highest[..., None]), 0.0)
    own_weight = jnp.exp(own_score - highest)
    denominator = jnp.sum(weights, axis=-1) + own_weight
    blended = jnp.einsum(
        "rgqt,rtgd->rgqd",
        weights.astype(jnp.bfloat16),
        cached_values,
        preferred_element_type=jnp.float32,
    )
    blended = blended + own_weight[..., None] * value_new.astype(jnp.float32)[:, :, None, :]
    return (
        (blended / denominator[..., None])
        .astype(jnp.bfloat16)
        .reshape(batch_rows, head_count * head_dim)
    )


def remote(src, dst, send_sem, recv_sem, device):
    return pltpu.make_async_remote_copy(
        src_ref=src,
        dst_ref=dst,
        send_sem=send_sem,
        recv_sem=recv_sem,
        device_id=device,
        device_id_type=MESH,
    )


def sums_kernel(
    nz, steps, x_ref, sq_ref, out_ref, sq_out_ref,
    core_recv, core_sq, send_buf, recv_buf, sq_send, sq_recv,
    core_ss, core_rs, csq_s, csq_r, z_ss, z_rs, zsq_ss, zsq_rs, fin_ss, fin_rs,
):
    me = lax.axis_index("wide")
    z, core = me // 2, lax.rem(me, 2)
    sibling = {"wide": me + 1 - 2 * core}
    rows, cols = x_ref.shape
    block = rows // nz
    half = cols // 2
    width = half // steps
    peers = [lax.rem(z + d, nz) for d in range(1, nz)]
    barrier = pltpu.get_barrier_semaphore()
    pl.semaphore_signal(barrier, inc=1, device_id=sibling, device_id_type=MESH)
    for peer in peers:
        pl.semaphore_signal(
            barrier, inc=1, device_id={"wide": peer * 2 + core}, device_id_type=MESH
        )
    pl.semaphore_wait(barrier, nz)

    def columns(which, t):
        return pl.ds(pl.multiple_of(which * half + t * width, 128), width)

    csq = remote(sq_ref, core_sq, csq_s, csq_r, sibling)
    csq.start()
    core_copies = []
    for t in range(steps):
        copy = remote(
            x_ref.at[:, columns(1 - core, t)],
            core_recv.at[t],
            core_ss.at[t],
            core_rs.at[t],
            sibling,
        )
        copy.start()
        core_copies.append(copy)
    copies = []
    csq.wait_recv()
    for d, peer in enumerate(peers):
        span = pl.ds(pl.multiple_of(peer * block, 8), block)
        sq_send[d] = sq_ref[span, :] + core_sq[span, :]
        copy = remote(
            sq_send.at[d], sq_recv.at[d], zsq_ss.at[d], zsq_rs.at[d], {"wide": peer * 2 + core}
        )
        copy.start()
        copies.append(copy)
    z_copies = []
    for t in range(steps):
        core_copies[t].wait_recv()
        row = []
        for d, peer in enumerate(peers):
            span = pl.ds(pl.multiple_of(peer * block, 8), block)
            both = x_ref[span, columns(core, t)] + core_recv[t, span, :]
            send_buf[t, d] = jnp.concatenate(
                [both[:, : width // 2], both[:, width // 2 :]], axis=0
            ).astype(jnp.bfloat16)
            copy = remote(
                send_buf.at[t, d],
                recv_buf.at[t, d],
                z_ss.at[t, d],
                z_rs.at[t, d],
                {"wide": peer * 2 + core},
            )
            copy.start()
            row.append(copy)
        z_copies.append(row)
    mine = pl.ds(pl.multiple_of(z * block, 8), block)
    total = sq_ref[mine, :] + core_sq[mine, :]
    for d in range(nz - 1):
        copies[d].wait_recv()
        total = total + sq_recv[d]
    sq_out_ref[...] = total
    finals = []
    for t in range(steps):
        acc = x_ref[mine, columns(core, t)] + core_recv[t, mine, :]
        left, right = acc[:, : width // 2], acc[:, width // 2 :]
        for d in range(nz - 1):
            z_copies[t][d].wait_recv()
            got = recv_buf[t, d].astype(jnp.float32)
            left = left + got[:block]
            right = right + got[block:]
        out_ref[:, columns(core, t)] = jnp.concatenate([left, right], axis=1)
        copy = remote(
            out_ref.at[:, columns(core, t)],
            out_ref.at[:, columns(core, t)],
            fin_ss.at[t],
            fin_rs.at[t],
            sibling,
        )
        copy.start()
        finals.append(copy)
    csq.wait_send()
    for copy in core_copies + copies + sum(z_copies, []):
        copy.wait_send()
    for t in range(steps):
        finals[t].wait_send()
        remote(
            out_ref.at[:, columns(1 - core, t)],
            out_ref.at[:, columns(1 - core, t)],
            fin_ss.at[t],
            fin_rs.at[t],
            sibling,
        ).wait_recv()


def sum_over_wide(x, sq, n_wide):
    nz = n_wide // 2
    rows, cols = x.shape
    block = rows // nz
    steps = 3
    width = cols // 2 // steps
    vmem = pl.BlockSpec(memory_space=pltpu.VMEM)
    dma = pltpu.SemaphoreType.DMA
    return pl.pallas_call(
        functools.partial(sums_kernel, nz, steps),
        out_shape=(
            jax.ShapeDtypeStruct((block, cols), jnp.float32),
            jax.ShapeDtypeStruct((block, 128), jnp.float32),
        ),
        in_specs=[vmem, vmem],
        out_specs=(vmem, vmem),
        scratch_shapes=[
            pltpu.VMEM((steps, rows, width), jnp.float32),
            pltpu.VMEM((rows, 128), jnp.float32),
            pltpu.VMEM((steps, nz - 1, 2 * block, width // 2), jnp.bfloat16),
            pltpu.VMEM((steps, nz - 1, 2 * block, width // 2), jnp.bfloat16),
            pltpu.VMEM((nz - 1, block, 128), jnp.float32),
            pltpu.VMEM((nz - 1, block, 128), jnp.float32),
            dma((steps,)),
            dma((steps,)),
            dma,
            dma,
            dma((steps, nz - 1)),
            dma((steps, nz - 1)),
            dma((nz - 1,)),
            dma((nz - 1,)),
            dma((steps,)),
            dma((steps,)),
        ],
        compiler_params=pltpu.CompilerParams(
            collective_id=0, has_side_effects=True, vmem_limit_bytes=48 << 20
        ),
    )(x, sq)


def project_kernel(
    nz, nn, own_rows, heads_ref, w_ref, out_ref,
    held, weights, parts, recv_parts,
    w_sem, right_s, left_s, right_r, left_r, sib_s, sib_r, x_ss, x_rs,
):
    me = lax.axis_index("wide")
    across = lax.axis_index("narrow")
    z, core = me // 2, lax.rem(me, 2)
    sib_index = me + 1 - 2 * core
    sibling = {"wide": sib_index}
    right, left = {"wide": me + 2}, {"wide": me - 2}
    has_right, has_left = z < nz - 1, z > 0
    n_wide = 2 * nz
    tiles = w_ref.shape[1] // TILE
    chunk = w_ref.shape[0] // PARTS
    out_rows = out_ref.shape[0]

    w_copies = []
    for t in range(tiles):
        cols = pl.ds(t * TILE, TILE)
        copy = pltpu.make_async_copy(w_ref.at[:, cols], weights.at[t], w_sem.at[t])
        copy.start()
        w_copies.append(copy)

    barrier = pltpu.get_barrier_semaphore()

    def greet(device):
        pl.semaphore_signal(barrier, inc=1, device_id=device, device_id_type=MESH)

    greet(sibling)
    for d in range(1, nn):
        greet({"narrow": lax.rem(across + d, nn)})

    @pl.when(has_right)
    def _():
        greet(right)

    @pl.when(has_left)
    def _():
        greet(left)

    ends = jnp.where(has_right, 1, 0) + jnp.where(has_left, 1, 0)
    pl.semaphore_wait(barrier, nn + ends)

    def to_right(h):
        slot = held.at[me - 2 * h]
        return remote(slot, slot, right_s.at[h], right_r.at[h], right)

    def to_left(h):
        slot = held.at[me + 2 * h]
        return remote(slot, slot, left_s.at[h], left_r.at[h], left)

    def to_sibling(k, index):
        return remote(held.at[index], held.at[index], sib_s.at[k], sib_r.at[k], sibling)

    held[me] = heads_ref[...]

    @pl.when(has_right)
    def _():
        to_right(0).start()

    @pl.when(has_left)
    def _():
        to_left(0).start()

    to_sibling(0, me).start()
    for h in range(1, nz):

        @pl.when(z - h >= 0)
        def _():
            slot = held.at[me - 2 * h]
            remote(slot, slot, right_s.at[h - 1], right_r.at[h - 1], left).wait_recv()

            @pl.when(has_right)
            def _():
                to_right(h).start()

            to_sibling(h, me - 2 * h).start()

        @pl.when(z + h < nz)
        def _():
            slot = held.at[me + 2 * h]
            remote(slot, slot, left_s.at[h - 1], left_r.at[h - 1], right).wait_recv()

            @pl.when(has_left)
            def _():
                to_left(h).start()

            to_sibling(nz - 1 + h, me + 2 * h).start()

    to_sibling(0, sib_index).wait_recv()
    for h in range(1, nz):

        @pl.when(z - h >= 0)
        def _():
            to_sibling(h, sib_index - 2 * h).wait_recv()

        @pl.when(z + h < nz)
        def _():
            to_sibling(nz - 1 + h, sib_index + 2 * h).wait_recv()

    for t in range(tiles):
        w_copies[t].wait()

    def exchange(d, t):
        to = lax.rem(across + d, nn)
        cols = pl.ds(pl.multiple_of(t * TILE, TILE), TILE)
        return remote(
            parts.at[to, :, cols],
            recv_parts.at[d - 1, :, cols],
            x_ss.at[d - 1, t],
            x_rs.at[d - 1, t],
            {"narrow": to},
        )

    def multiply(t, carry):
        acc = jnp.zeros((n_wide * PAD, TILE), jnp.float32)
        for q in range(PARTS):
            lhs = held[:, q].reshape(n_wide * PAD, chunk)
            acc = acc + jnp.dot(
                lhs,
                weights[t, pl.ds(q * chunk, chunk), :],
                preferred_element_type=jnp.float32,
            )
        dense = jnp.concatenate(
            [acc[b * PAD : b * PAD + own_rows] for b in range(n_wide)], axis=0
        ).astype(jnp.bfloat16)
        cols = pl.ds(pl.multiple_of(t * TILE, TILE), TILE)
        for p in range(nn):
            parts[p, :, cols] = dense[p * out_rows : (p + 1) * out_rows]
        for d in range(1, nn):
            exchange(d, t).start()
        return carry

    lax.fori_loop(0, tiles, multiply, 0)

    def finish(t, carry):
        cols = pl.ds(pl.multiple_of(t * TILE, TILE), TILE)
        total = parts[across, :, cols].astype(jnp.float32)
        for d in range(1, nn):
            exchange(d, t).wait_recv()
            total = total + recv_parts[d - 1, :, cols].astype(jnp.float32)
        out_ref[:, cols] = total.astype(jnp.bfloat16)
        for d in range(1, nn):
            exchange(d, t).wait_send()
        return carry

    lax.fori_loop(0, tiles, finish, 0)

    to_sibling(0, me).wait_send()
    for h in range(nz):

        @pl.when(jnp.logical_and(z - h >= 0, has_right))
        def _():
            to_right(h).wait_send()

        @pl.when(jnp.logical_and(z + h < nz, has_left))
        def _():
            to_left(h).wait_send()

        if h > 0:

            @pl.when(z - h >= 0)
            def _():
                to_sibling(h, me - 2 * h).wait_send()

            @pl.when(z + h < nz)
            def _():
                to_sibling(nz - 1 + h, me + 2 * h).wait_send()


def project(heads, w_out, n_wide, nn, own_rows):
    nz = n_wide // 2
    depth, cols = w_out.shape
    chunk = depth // PARTS
    tiles = cols // TILE
    out_rows = n_wide * own_rows // nn
    dma = pltpu.SemaphoreType.DMA
    return pl.pallas_call(
        functools.partial(project_kernel, nz, nn, own_rows),
        out_shape=jax.ShapeDtypeStruct((out_rows, cols), jnp.bfloat16),
        in_specs=[
            pl.BlockSpec(memory_space=pltpu.VMEM),
            pl.BlockSpec(memory_space=pl.ANY),
        ],
        out_specs=pl.BlockSpec(memory_space=pltpu.VMEM),
        scratch_shapes=[
            pltpu.VMEM((n_wide, PARTS, PAD, chunk), jnp.bfloat16),
            pltpu.VMEM((tiles, depth, TILE), jnp.bfloat16),
            pltpu.VMEM((nn, out_rows, cols), jnp.bfloat16),
            pltpu.VMEM((nn - 1, out_rows, cols), jnp.bfloat16),
            dma((tiles,)),
            dma((nz,)),
            dma((nz,)),
            dma((nz,)),
            dma((nz,)),
            dma((2 * nz - 1,)),
            dma((2 * nz - 1,)),
            dma((nn - 1, tiles)),
            dma((nn - 1, tiles)),
        ],
        compiler_params=pltpu.CompilerParams(
            collective_id=1, has_side_effects=True, vmem_limit_bytes=56 << 20
        ),
    )(heads, w_out)


def per_device(
    n_wide, nn, tokens, norm_gain, w_query, w_key, w_value, w_out, cache_key, cache_value, lengths
):
    all_rows = lax.all_gather(tokens, "narrow", axis=0, tiled=True)
    features = all_rows.astype(jnp.float32)
    squares = jnp.sum(features * features, axis=1)
    scaled = (features * norm_gain.astype(jnp.float32)[None, :]).astype(jnp.bfloat16)
    own_rows = cache_key.shape[0]
    index = lax.axis_index("wide")
    row_start = index * own_rows
    query_cols = w_query.shape[1]
    kv_cols = w_key.shape[1]
    partial_sums = jnp.concatenate(
        [
            jnp.dot(scaled, w_query, preferred_element_type=jnp.float32),
            jnp.dot(scaled, w_key, preferred_element_type=jnp.float32),
            jnp.dot(scaled, w_value, preferred_element_type=jnp.float32),
        ],
        axis=1,
    )
    chip_sums, chip_squares = sum_over_wide(
        partial_sums, jnp.broadcast_to(squares[:, None], (squares.shape[0], 128)), n_wide
    )
    chip_start = lax.rem(index, 2) * own_rows
    summed = lax.dynamic_slice_in_dim(chip_sums, chip_start, own_rows, 0)
    mean = lax.dynamic_slice_in_dim(chip_squares, chip_start, own_rows, 0)[:, :1] / D
    summed = summed * lax.rsqrt(mean + norm_eps)
    own_lengths = lax.dynamic_slice_in_dim(lengths, row_start, own_rows, 0)
    queries = rotate(
        summed[:, :query_cols].reshape(own_rows, query_cols // HD, HD), own_lengths
    ).astype(jnp.bfloat16)
    key_new = rotate(
        summed[:, query_cols : query_cols + kv_cols].reshape(own_rows, kv_cols // HD, HD),
        own_lengths,
    ).astype(jnp.bfloat16)
    value_new = (
        summed[:, query_cols + kv_cols :].reshape(own_rows, kv_cols // HD, HD).astype(jnp.bfloat16)
    )
    heads_out = attend(queries, key_new, value_new, cache_key, cache_value, own_lengths)
    stacked = jnp.stack(jnp.split(heads_out, PARTS, axis=1), axis=0)
    stacked = jnp.pad(stacked, ((0, 0), (0, PAD - own_rows), (0, 0)))
    return project(stacked, w_out, n_wide, nn, own_rows)


def solution(mesh):
    return jax.shard_map(
        functools.partial(per_device, mesh.shape["wide"], mesh.shape["narrow"]),
        mesh=mesh,
        in_specs=(
            P(("groups", "narrow"), "wide"),
            P("wide"),
            P("wide", "narrow"),
            P("wide", "narrow"),
            P("wide", "narrow"),
            P("narrow", "wide"),
            P(("groups", "wide"), None, "narrow"),
            P(("groups", "wide"), None, "narrow"),
            P("groups"),
        ),
        out_specs=P(("groups", "narrow"), "wide"),
        check_vma=False,
    )
```

```python
import functools

import jax
import jax.numpy as jnp
from jax import lax
from jax.experimental import pallas as pl
from jax.experimental.pallas import tpu as pltpu
from jax.sharding import PartitionSpec as P

D = 16384
HD = 128
PAD = 16
PARTS = 4
TILE = 256
MESH = pl.DeviceIdType.MESH


rope_base = 500000.0
norm_eps = 1e-05


def rotate(vectors, positions):
    half_dim = vectors.shape[-1] // 2
    frequency = rope_base ** (-jnp.arange(half_dim, dtype=jnp.float32) / half_dim)
    angles = positions.astype(jnp.float32)[:, None] * frequency[None, :]
    cosine = jnp.cos(angles)[:, None, :]
    sines = jnp.sin(angles)[:, None, :]
    leading_half = vectors[..., :half_dim]
    trailing_half = vectors[..., half_dim:]
    return jnp.concatenate(
        [
            leading_half * cosine - trailing_half * sines,
            trailing_half * cosine + leading_half * sines,
        ],
        axis=-1,
    )


def attend(queries, key_new, value_new, cache_key, cache_value, lengths):
    batch_rows, head_count, head_dim = queries.shape
    group_count = key_new.shape[1]
    per_group = head_count // group_count
    token_count = cache_key.shape[1]
    grouped = queries.reshape(batch_rows, group_count, per_group, head_dim)
    cached_keys = cache_key.reshape(batch_rows, token_count, group_count, head_dim)
    cached_values = cache_value.reshape(batch_rows, token_count, group_count, head_dim)
    score_scale = head_dim ** (-0.5)
    scores = (
        jnp.einsum("rgqd,rtgd->rgqt", grouped, cached_keys, preferred_element_type=jnp.float32)
        * score_scale
    )
    own_score = (
        jnp.einsum("rgqd,rgd->rgq", grouped, key_new, preferred_element_type=jnp.float32)
        * score_scale
    )
    usable = (jnp.arange(token_count)[None, :] < lengths[:, None])[:, None, None, :]
    highest = jnp.maximum(jnp.max(jnp.where(usable, scores, -1e30), axis=-1), own_score)
    weights = jnp.where(usable, jnp.exp(scores - highest[..., None]), 0.0)
    own_weight = jnp.exp(own_score - highest)
    denominator = jnp.sum(weights, axis=-1) + own_weight
    blended = jnp.einsum(
        "rgqt,rtgd->rgqd",
        weights.astype(jnp.bfloat16),
        cached_values,
        preferred_element_type=jnp.float32,
    )
    blended = blended + own_weight[..., None] * value_new.astype(jnp.float32)[:, :, None, :]
    return (
        (blended / denominator[..., None])
        .astype(jnp.bfloat16)
        .reshape(batch_rows, head_count * head_dim)
    )


def remote(src, dst, send_sem, recv_sem, device):
    return pltpu.make_async_remote_copy(
        src_ref=src,
        dst_ref=dst,
        send_sem=send_sem,
        recv_sem=recv_sem,
        device_id=device,
        device_id_type=MESH,
    )


def sums_kernel(
    nz, nn, steps, tok_ref, gain_ref, wq_ref, wk_ref, wv_ref, out_ref, sq_out_ref,
    tok, scaled, sq, weights, x, core_recv, core_sq, send_buf, recv_buf, sq_send, sq_recv,
    tok_s, tok_r, w_sem, core_ss, core_rs, csq_s, csq_r, z_ss, z_rs, zsq_ss, zsq_rs, fin_ss, fin_rs,
):
    me = lax.axis_index("wide")
    across = lax.axis_index("narrow")
    z, core = me // 2, lax.rem(me, 2)
    away = 1 - core
    sibling = {"wide": me + 1 - 2 * core}
    part_rows = tok_ref.shape[0]
    rows = part_rows * nn
    width = wk_ref.shape[1]
    block = rows // nz
    peers = [lax.rem(z + d, nz) for d in range(1, nz)]

    def query_weights(t, which):
        start = pl.multiple_of((which * (steps - 1) + t) * width, 128)
        return pltpu.make_async_copy(
            wq_ref.at[:, pl.ds(start, width)], weights.at[t, which], w_sem.at[t, which]
        )

    for t in range(steps - 1):
        query_weights(t, away).start()
        query_weights(t, core).start()
    last = steps - 1
    pltpu.make_async_copy(wk_ref, weights.at[last, 0], w_sem.at[last, 0]).start()
    pltpu.make_async_copy(wv_ref, weights.at[last, 1], w_sem.at[last, 1]).start()

    barrier = pltpu.get_barrier_semaphore()

    def greet(device):
        pl.semaphore_signal(barrier, inc=1, device_id=device, device_id_type=MESH)

    greet(sibling)
    for peer in peers:
        greet({"wide": peer * 2 + core})
    for d in range(1, nn):
        greet({"narrow": lax.rem(across + d, nn)})
    pl.semaphore_wait(barrier, nz + nn - 1)

    tok_copies = []
    for d in range(1, nn):
        copy = remote(
            tok_ref,
            tok.at[d - 1],
            tok_s.at[d - 1],
            tok_r.at[d - 1],
            {"narrow": lax.rem(across + d, nn)},
        )
        copy.start()
        tok_copies.append(copy)

    def take(values, origin):
        features = values.astype(jnp.float32)
        span = pl.ds(pl.multiple_of(origin * part_rows, 16), part_rows)
        total = jnp.sum(features * features, axis=1, keepdims=True)
        sq[span, :] = jnp.broadcast_to(total, (part_rows, 128))
        scaled[span, :] = (features * gain_ref[...].astype(jnp.float32)).astype(jnp.bfloat16)

    take(tok_ref[...], across)
    for d in range(1, nn):
        tok_copies[d - 1].wait_recv()
        take(tok[d - 1], lax.rem(across + nn - d, nn))

    csq = remote(sq, core_sq, csq_s, csq_r, sibling)
    csq.start()

    def to_core(t):
        return remote(x.at[t, away], core_recv.at[t], core_ss.at[t], core_rs.at[t], sibling)

    def to_chip(t, d):
        return remote(
            send_buf.at[t, d],
            recv_buf.at[t, d],
            z_ss.at[t, d],
            z_rs.at[t, d],
            {"wide": peers[d] * 2 + core},
        )

    def final(t, which):
        return remote(
            out_ref.at[t, which], out_ref.at[t, which], fin_ss.at[t], fin_rs.at[t], sibling
        )

    def multiply(t, which):
        pltpu.make_async_copy(
            wq_ref.at[:, pl.ds(0, width)], weights.at[t, which], w_sem.at[t, which]
        ).wait()
        x[t, which] = jnp.dot(
            scaled[...], weights[t, which], preferred_element_type=jnp.float32
        )

    def forward(t):
        to_core(t).wait_recv()
        for d, peer in enumerate(peers):
            span = pl.ds(pl.multiple_of(peer * block, 8), block)
            both = x[t, core, span, :] + core_recv[t, span, :]
            send_buf[t, d] = jnp.concatenate(
                [both[:, : width // 2], both[:, width // 2 :]], axis=0
            ).astype(jnp.bfloat16)
            to_chip(t, d).start()

    def step(t, carry):
        multiply(t, away)
        to_core(t).start()
        multiply(t, core)

        @pl.when(t > 0)
        def _():
            forward(t - 1)

        return carry

    lax.fori_loop(0, steps, step, 0)
    forward(steps - 1)

    csq.wait_recv()
    sq_copies = []
    for d, peer in enumerate(peers):
        span = pl.ds(pl.multiple_of(peer * block, 8), block)
        sq_send[d] = sq[span, :] + core_sq[span, :]
        copy = remote(
            sq_send.at[d], sq_recv.at[d], zsq_ss.at[d], zsq_rs.at[d], {"wide": peer * 2 + core}
        )
        copy.start()
        sq_copies.append(copy)
    mine = pl.ds(pl.multiple_of(z * block, 8), block)

    def collect(t, carry):
        acc = x[t, core, mine, :] + core_recv[t, mine, :]
        left, right = acc[:, : width // 2], acc[:, width // 2 :]
        for d in range(nz - 1):
            to_chip(t, d).wait_recv()
            got = recv_buf[t, d].astype(jnp.float32)
            left = left + got[:block]
            right = right + got[block:]
        out_ref[t, core] = jnp.concatenate([left, right], axis=1)
        final(t, core).start()
        return carry

    lax.fori_loop(0, steps, collect, 0)
    total = sq[mine, :] + core_sq[mine, :]
    for d in range(nz - 1):
        sq_copies[d].wait_recv()
        total = total + sq_recv[d]
    sq_out_ref[...] = total

    def drain(t, carry):
        to_core(t).wait_send()
        for d in range(nz - 1):
            to_chip(t, d).wait_send()
        final(t, core).wait_send()
        final(t, away).wait_recv()
        return carry

    lax.fori_loop(0, steps, drain, 0)
    csq.wait_send()
    for copy in tok_copies + sq_copies:
        copy.wait_send()


def project_in(tokens, norm_gain, w_query, w_key, w_value, n_wide, nn):
    nz = n_wide // 2
    part_rows, depth = tokens.shape
    rows = part_rows * nn
    block = rows // nz
    width = w_key.shape[1]
    steps = w_query.shape[1] // (2 * width) + 1
    vmem = pl.BlockSpec(memory_space=pltpu.VMEM)
    hbm = pl.BlockSpec(memory_space=pl.ANY)
    dma = pltpu.SemaphoreType.DMA
    return pl.pallas_call(
        functools.partial(sums_kernel, nz, nn, steps),
        out_shape=(
            jax.ShapeDtypeStruct((steps, 2, block, width), jnp.float32),
            jax.ShapeDtypeStruct((block, 128), jnp.float32),
        ),
        in_specs=[vmem, vmem, hbm, hbm, hbm],
        out_specs=(vmem, vmem),
        scratch_shapes=[
            pltpu.VMEM((nn - 1, part_rows, depth), jnp.bfloat16),
            pltpu.VMEM((rows, depth), jnp.bfloat16),
            pltpu.VMEM((rows, 128), jnp.float32),
            pltpu.VMEM((steps, 2, depth, width), jnp.bfloat16),
            pltpu.VMEM((steps, 2, rows, width), jnp.float32),
            pltpu.VMEM((steps, rows, width), jnp.float32),
            pltpu.VMEM((rows, 128), jnp.float32),
            pltpu.VMEM((steps, nz - 1, 2 * block, width // 2), jnp.bfloat16),
            pltpu.VMEM((steps, nz - 1, 2 * block, width // 2), jnp.bfloat16),
            pltpu.VMEM((nz - 1, block, 128), jnp.float32),
            pltpu.VMEM((nz - 1, block, 128), jnp.float32),
            dma((nn - 1,)),
            dma((nn - 1,)),
            dma((steps, 2)),
            dma((steps,)),
            dma((steps,)),
            dma,
            dma,
            dma((steps, nz - 1)),
            dma((steps, nz - 1)),
            dma((nz - 1,)),
            dma((nz - 1,)),
            dma((steps,)),
            dma((steps,)),
        ],
        compiler_params=pltpu.CompilerParams(
            collective_id=0, has_side_effects=True, vmem_limit_bytes=56 << 20
        ),
    )(tokens, norm_gain[None, :], w_query, w_key, w_value)


def project_kernel(
    nz, nn, own_rows, heads_ref, w_ref, out_ref,
    held, weights, parts, recv_parts,
    w_sem, right_s, left_s, right_r, left_r, sib_s, sib_r, x_ss, x_rs,
):
    me = lax.axis_index("wide")
    across = lax.axis_index("narrow")
    z, core = me // 2, lax.rem(me, 2)
    sib_index = me + 1 - 2 * core
    sibling = {"wide": sib_index}
    right, left = {"wide": me + 2}, {"wide": me - 2}
    has_right, has_left = z < nz - 1, z > 0
    n_wide = 2 * nz
    tiles = w_ref.shape[1] // TILE
    chunk = w_ref.shape[0] // PARTS
    out_rows = out_ref.shape[0]

    w_copies = []
    for t in range(tiles):
        cols = pl.ds(t * TILE, TILE)
        copy = pltpu.make_async_copy(w_ref.at[:, cols], weights.at[t], w_sem.at[t])
        copy.start()
        w_copies.append(copy)

    barrier = pltpu.get_barrier_semaphore()

    def greet(device):
        pl.semaphore_signal(barrier, inc=1, device_id=device, device_id_type=MESH)

    greet(sibling)
    for d in range(1, nn):
        greet({"narrow": lax.rem(across + d, nn)})

    @pl.when(has_right)
    def _():
        greet(right)

    @pl.when(has_left)
    def _():
        greet(left)

    ends = jnp.where(has_right, 1, 0) + jnp.where(has_left, 1, 0)
    pl.semaphore_wait(barrier, nn + ends)

    def to_right(h):
        slot = held.at[me - 2 * h]
        return remote(slot, slot, right_s.at[h], right_r.at[h], right)

    def to_left(h):
        slot = held.at[me + 2 * h]
        return remote(slot, slot, left_s.at[h], left_r.at[h], left)

    def to_sibling(k, index):
        return remote(held.at[index], held.at[index], sib_s.at[k], sib_r.at[k], sibling)

    held[me] = heads_ref[...]

    @pl.when(has_right)
    def _():
        to_right(0).start()

    @pl.when(has_left)
    def _():
        to_left(0).start()

    to_sibling(0, me).start()
    for h in range(1, nz):

        @pl.when(z - h >= 0)
        def _():
            slot = held.at[me - 2 * h]
            remote(slot, slot, right_s.at[h - 1], right_r.at[h - 1], left).wait_recv()

            @pl.when(has_right)
            def _():
                to_right(h).start()

            to_sibling(h, me - 2 * h).start()

        @pl.when(z + h < nz)
        def _():
            slot = held.at[me + 2 * h]
            remote(slot, slot, left_s.at[h - 1], left_r.at[h - 1], right).wait_recv()

            @pl.when(has_left)
            def _():
                to_left(h).start()

            to_sibling(nz - 1 + h, me + 2 * h).start()

    to_sibling(0, sib_index).wait_recv()
    for h in range(1, nz):

        @pl.when(z - h >= 0)
        def _():
            to_sibling(h, sib_index - 2 * h).wait_recv()

        @pl.when(z + h < nz)
        def _():
            to_sibling(nz - 1 + h, sib_index + 2 * h).wait_recv()

    for t in range(tiles):
        w_copies[t].wait()

    def exchange(d, t):
        to = lax.rem(across + d, nn)
        cols = pl.ds(pl.multiple_of(t * TILE, TILE), TILE)
        return remote(
            parts.at[to, :, cols],
            recv_parts.at[d - 1, :, cols],
            x_ss.at[d - 1, t],
            x_rs.at[d - 1, t],
            {"narrow": to},
        )

    def multiply(t, carry):
        acc = jnp.zeros((n_wide * PAD, TILE), jnp.float32)
        for q in range(PARTS):
            lhs = held[:, q].reshape(n_wide * PAD, chunk)
            acc = acc + jnp.dot(
                lhs,
                weights[t, pl.ds(q * chunk, chunk), :],
                preferred_element_type=jnp.float32,
            )
        dense = jnp.concatenate(
            [acc[b * PAD : b * PAD + own_rows] for b in range(n_wide)], axis=0
        ).astype(jnp.bfloat16)
        cols = pl.ds(pl.multiple_of(t * TILE, TILE), TILE)
        for p in range(nn):
            parts[p, :, cols] = dense[p * out_rows : (p + 1) * out_rows]
        for d in range(1, nn):
            exchange(d, t).start()
        return carry

    lax.fori_loop(0, tiles, multiply, 0)

    def finish(t, carry):
        cols = pl.ds(pl.multiple_of(t * TILE, TILE), TILE)
        total = parts[across, :, cols].astype(jnp.float32)
        for d in range(1, nn):
            exchange(d, t).wait_recv()
            total = total + recv_parts[d - 1, :, cols].astype(jnp.float32)
        out_ref[:, cols] = total.astype(jnp.bfloat16)
        for d in range(1, nn):
            exchange(d, t).wait_send()
        return carry

    lax.fori_loop(0, tiles, finish, 0)

    to_sibling(0, me).wait_send()
    for h in range(nz):

        @pl.when(jnp.logical_and(z - h >= 0, has_right))
        def _():
            to_right(h).wait_send()

        @pl.when(jnp.logical_and(z + h < nz, has_left))
        def _():
            to_left(h).wait_send()

        if h > 0:

            @pl.when(z - h >= 0)
            def _():
                to_sibling(h, me - 2 * h).wait_send()

            @pl.when(z + h < nz)
            def _():
                to_sibling(nz - 1 + h, me + 2 * h).wait_send()


def project(heads, w_out, n_wide, nn, own_rows):
    nz = n_wide // 2
    depth, cols = w_out.shape
    chunk = depth // PARTS
    tiles = cols // TILE
    out_rows = n_wide * own_rows // nn
    dma = pltpu.SemaphoreType.DMA
    return pl.pallas_call(
        functools.partial(project_kernel, nz, nn, own_rows),
        out_shape=jax.ShapeDtypeStruct((out_rows, cols), jnp.bfloat16),
        in_specs=[
            pl.BlockSpec(memory_space=pltpu.VMEM),
            pl.BlockSpec(memory_space=pl.ANY),
        ],
        out_specs=pl.BlockSpec(memory_space=pltpu.VMEM),
        scratch_shapes=[
            pltpu.VMEM((n_wide, PARTS, PAD, chunk), jnp.bfloat16),
            pltpu.VMEM((tiles, depth, TILE), jnp.bfloat16),
            pltpu.VMEM((nn, out_rows, cols), jnp.bfloat16),
            pltpu.VMEM((nn - 1, out_rows, cols), jnp.bfloat16),
            dma((tiles,)),
            dma((nz,)),
            dma((nz,)),
            dma((nz,)),
            dma((nz,)),
            dma((2 * nz - 1,)),
            dma((2 * nz - 1,)),
            dma((nn - 1, tiles)),
            dma((nn - 1, tiles)),
        ],
        compiler_params=pltpu.CompilerParams(
            collective_id=1, has_side_effects=True, vmem_limit_bytes=56 << 20
        ),
    )(heads, w_out)


def per_device(
    n_wide, nn, tokens, norm_gain, w_query, w_key, w_value, w_out, cache_key, cache_value, lengths
):
    own_rows = cache_key.shape[0]
    index = lax.axis_index("wide")
    row_start = index * own_rows
    query_cols = w_query.shape[1]
    kv_cols = w_key.shape[1]
    chip_sums, chip_squares = project_in(
        tokens, norm_gain, w_query, w_key, w_value, n_wide, nn
    )
    chip_start = lax.rem(index, 2) * own_rows
    mean = lax.dynamic_slice_in_dim(chip_squares, chip_start, own_rows, 0)[:, :1] / D
    own_sums = lax.dynamic_slice_in_dim(chip_sums, chip_start, own_rows, 2)
    last = own_sums.shape[0] - 1
    summed = jnp.concatenate(
        [
            own_sums[:last].transpose(2, 1, 0, 3).reshape(own_rows, query_cols),
            own_sums[last].transpose(1, 0, 2).reshape(own_rows, 2 * kv_cols),
        ],
        axis=1,
    )
    summed = summed * lax.rsqrt(mean + norm_eps)
    own_lengths = lax.dynamic_slice_in_dim(lengths, row_start, own_rows, 0)
    queries = rotate(
        summed[:, :query_cols].reshape(own_rows, query_cols // HD, HD), own_lengths
    ).astype(jnp.bfloat16)
    key_new = rotate(
        summed[:, query_cols : query_cols + kv_cols].reshape(own_rows, kv_cols // HD, HD),
        own_lengths,
    ).astype(jnp.bfloat16)
    value_new = (
        summed[:, query_cols + kv_cols :].reshape(own_rows, kv_cols // HD, HD).astype(jnp.bfloat16)
    )
    heads_out = attend(queries, key_new, value_new, cache_key, cache_value, own_lengths)
    stacked = jnp.stack(jnp.split(heads_out, PARTS, axis=1), axis=0)
    stacked = jnp.pad(stacked, ((0, 0), (0, PAD - own_rows), (0, 0)))
    return project(stacked, w_out, n_wide, nn, own_rows)


def solution(mesh):
    return jax.shard_map(
        functools.partial(per_device, mesh.shape["wide"], mesh.shape["narrow"]),
        mesh=mesh,
        in_specs=(
            P(("groups", "narrow"), "wide"),
            P("wide"),
            P("wide", "narrow"),
            P("wide", "narrow"),
            P("wide", "narrow"),
            P("narrow", "wide"),
            P(("groups", "wide"), None, "narrow"),
            P(("groups", "wide"), None, "narrow"),
            P("groups"),
        ),
        out_specs=P(("groups", "narrow"), "wide"),
        check_vma=False,
    )
```

```python
import functools

import jax
import jax.numpy as jnp
from jax import lax
from jax.experimental import pallas as pl
from jax.experimental.pallas import tpu as pltpu
from jax.sharding import PartitionSpec as P

D = 16384
HD = 128
PARTS = 4
CHUNKS = 4
TILE = 256
MESH = pl.DeviceIdType.MESH


rope_base = 500000.0
norm_eps = 1e-05


def rotate(vectors, positions):
    half_dim = vectors.shape[-1] // 2
    frequency = rope_base ** (-jnp.arange(half_dim, dtype=jnp.float32) / half_dim)
    angles = positions.astype(jnp.float32)[:, None] * frequency[None, :]
    cosine = jnp.cos(angles)[:, None, :]
    sines = jnp.sin(angles)[:, None, :]
    leading_half = vectors[..., :half_dim]
    trailing_half = vectors[..., half_dim:]
    return jnp.concatenate(
        [
            leading_half * cosine - trailing_half * sines,
            trailing_half * cosine + leading_half * sines,
        ],
        axis=-1,
    )


def attend(queries, key_new, value_new, cache_key, cache_value, lengths):
    batch_rows, head_count, head_dim = queries.shape
    group_count = key_new.shape[1]
    per_group = head_count // group_count
    token_count = cache_key.shape[1]
    grouped = queries.reshape(batch_rows, group_count, per_group, head_dim)
    cached_keys = cache_key.reshape(batch_rows, token_count, group_count, head_dim)
    cached_values = cache_value.reshape(batch_rows, token_count, group_count, head_dim)
    score_scale = head_dim ** (-0.5)
    scores = (
        jnp.einsum("rgqd,rtgd->rgqt", grouped, cached_keys, preferred_element_type=jnp.float32)
        * score_scale
    )
    own_score = (
        jnp.einsum("rgqd,rgd->rgq", grouped, key_new, preferred_element_type=jnp.float32)
        * score_scale
    )
    usable = (jnp.arange(token_count)[None, :] < lengths[:, None])[:, None, None, :]
    highest = jnp.maximum(jnp.max(jnp.where(usable, scores, -1e30), axis=-1), own_score)
    weights = jnp.where(usable, jnp.exp(scores - highest[..., None]), 0.0)
    own_weight = jnp.exp(own_score - highest)
    denominator = jnp.sum(weights, axis=-1) + own_weight
    blended = jnp.einsum(
        "rgqt,rtgd->rgqd",
        weights.astype(jnp.bfloat16),
        cached_values,
        preferred_element_type=jnp.float32,
    )
    blended = blended + own_weight[..., None] * value_new.astype(jnp.float32)[:, :, None, :]
    return (
        (blended / denominator[..., None])
        .astype(jnp.bfloat16)
        .reshape(batch_rows, head_count * head_dim)
    )


def remote(src, dst, send_sem, recv_sem, device):
    return pltpu.make_async_remote_copy(
        src_ref=src,
        dst_ref=dst,
        send_sem=send_sem,
        recv_sem=recv_sem,
        device_id=device,
        device_id_type=MESH,
    )


def sums_kernel(
    nz, nn, steps, tok_ref, gain_ref, wq_ref, wk_ref, wv_ref, out_ref, sq_out_ref,
    tok, scaled, sq, weights, x, core_recv, core_sq, send_buf, recv_buf, sq_send, sq_recv,
    tok_s, tok_r, w_sem, core_ss, core_rs, csq_s, csq_r, z_ss, z_rs, zsq_ss, zsq_rs, fin_ss, fin_rs,
):
    me = lax.axis_index("wide")
    across = lax.axis_index("narrow")
    z, core = me // 2, lax.rem(me, 2)
    away = 1 - core
    sibling = {"wide": me + 1 - 2 * core}
    part_rows = tok_ref.shape[0]
    rows = part_rows * nn
    width = wk_ref.shape[1]
    block = rows // nz
    peers = [lax.rem(z + d, nz) for d in range(1, nz)]

    def query_weights(t, which):
        start = pl.multiple_of((which * (steps - 1) + t) * width, 128)
        return pltpu.make_async_copy(
            wq_ref.at[:, pl.ds(start, width)], weights.at[t, which], w_sem.at[t, which]
        )

    for t in range(steps - 1):
        query_weights(t, away).start()
        query_weights(t, core).start()
    last = steps - 1
    pltpu.make_async_copy(wk_ref, weights.at[last, 0], w_sem.at[last, 0]).start()
    pltpu.make_async_copy(wv_ref, weights.at[last, 1], w_sem.at[last, 1]).start()

    barrier = pltpu.get_barrier_semaphore()

    def greet(device):
        pl.semaphore_signal(barrier, inc=1, device_id=device, device_id_type=MESH)

    greet(sibling)
    for peer in peers:
        greet({"wide": peer * 2 + core})
    for d in range(1, nn):
        greet({"narrow": lax.rem(across + d, nn)})
    pl.semaphore_wait(barrier, nz + nn - 1)

    tok_copies = []
    for d in range(1, nn):
        copy = remote(
            tok_ref,
            tok.at[d - 1],
            tok_s.at[d - 1],
            tok_r.at[d - 1],
            {"narrow": lax.rem(across + d, nn)},
        )
        copy.start()
        tok_copies.append(copy)

    def take(values, origin):
        features = values.astype(jnp.float32)
        span = pl.ds(pl.multiple_of(origin * part_rows, 16), part_rows)
        total = jnp.sum(features * features, axis=1, keepdims=True)
        sq[span, :] = jnp.broadcast_to(total, (part_rows, 128))
        scaled[span, :] = (features * gain_ref[...].astype(jnp.float32)).astype(jnp.bfloat16)

    take(tok_ref[...], across)
    for d in range(1, nn):
        tok_copies[d - 1].wait_recv()
        take(tok[d - 1], lax.rem(across + nn - d, nn))

    csq = remote(sq, core_sq, csq_s, csq_r, sibling)
    csq.start()

    def to_core(t):
        return remote(x.at[t, away], core_recv.at[t], core_ss.at[t], core_rs.at[t], sibling)

    def to_chip(t, d):
        return remote(
            send_buf.at[t, d],
            recv_buf.at[t, d],
            z_ss.at[t, d],
            z_rs.at[t, d],
            {"wide": peers[d] * 2 + core},
        )

    def final(t, which):
        return remote(
            out_ref.at[t, which], out_ref.at[t, which], fin_ss.at[t], fin_rs.at[t], sibling
        )

    def multiply(t, which):
        pltpu.make_async_copy(
            wq_ref.at[:, pl.ds(0, width)], weights.at[t, which], w_sem.at[t, which]
        ).wait()
        x[t, which] = jnp.dot(
            scaled[...], weights[t, which], preferred_element_type=jnp.float32
        )

    def forward(t):
        to_core(t).wait_recv()
        for d, peer in enumerate(peers):
            span = pl.ds(pl.multiple_of(peer * block, 8), block)
            both = x[t, core, span, :] + core_recv[t, span, :]
            send_buf[t, d] = jnp.concatenate(
                [both[:, : width // 2], both[:, width // 2 :]], axis=0
            ).astype(jnp.bfloat16)
            to_chip(t, d).start()

    def step(t, carry):
        multiply(t, away)
        to_core(t).start()
        multiply(t, core)

        @pl.when(t > 0)
        def _():
            forward(t - 1)

        return carry

    lax.fori_loop(0, steps, step, 0)
    forward(steps - 1)

    csq.wait_recv()
    sq_copies = []
    for d, peer in enumerate(peers):
        span = pl.ds(pl.multiple_of(peer * block, 8), block)
        sq_send[d] = sq[span, :] + core_sq[span, :]
        copy = remote(
            sq_send.at[d], sq_recv.at[d], zsq_ss.at[d], zsq_rs.at[d], {"wide": peer * 2 + core}
        )
        copy.start()
        sq_copies.append(copy)
    mine = pl.ds(pl.multiple_of(z * block, 8), block)

    def collect(t, carry):
        acc = x[t, core, mine, :] + core_recv[t, mine, :]
        left, right = acc[:, : width // 2], acc[:, width // 2 :]
        for d in range(nz - 1):
            to_chip(t, d).wait_recv()
            got = recv_buf[t, d].astype(jnp.float32)
            left = left + got[:block]
            right = right + got[block:]
        out_ref[t, core] = jnp.concatenate([left, right], axis=1)
        final(t, core).start()
        return carry

    lax.fori_loop(0, steps, collect, 0)
    total = sq[mine, :] + core_sq[mine, :]
    for d in range(nz - 1):
        sq_copies[d].wait_recv()
        total = total + sq_recv[d]
    sq_out_ref[...] = total

    def drain(t, carry):
        to_core(t).wait_send()
        for d in range(nz - 1):
            to_chip(t, d).wait_send()
        final(t, core).wait_send()
        final(t, away).wait_recv()
        return carry

    lax.fori_loop(0, steps, drain, 0)
    csq.wait_send()
    for copy in tok_copies + sq_copies:
        copy.wait_send()


def project_in(tokens, norm_gain, w_query, w_key, w_value, n_wide, nn):
    nz = n_wide // 2
    part_rows, depth = tokens.shape
    rows = part_rows * nn
    block = rows // nz
    width = w_key.shape[1]
    steps = w_query.shape[1] // (2 * width) + 1
    vmem = pl.BlockSpec(memory_space=pltpu.VMEM)
    hbm = pl.BlockSpec(memory_space=pl.ANY)
    dma = pltpu.SemaphoreType.DMA
    return pl.pallas_call(
        functools.partial(sums_kernel, nz, nn, steps),
        out_shape=(
            jax.ShapeDtypeStruct((steps, 2, block, width), jnp.float32),
            jax.ShapeDtypeStruct((block, 128), jnp.float32),
        ),
        in_specs=[vmem, vmem, hbm, hbm, hbm],
        out_specs=(vmem, vmem),
        scratch_shapes=[
            pltpu.VMEM((nn - 1, part_rows, depth), jnp.bfloat16),
            pltpu.VMEM((rows, depth), jnp.bfloat16),
            pltpu.VMEM((rows, 128), jnp.float32),
            pltpu.VMEM((steps, 2, depth, width), jnp.bfloat16),
            pltpu.VMEM((steps, 2, rows, width), jnp.float32),
            pltpu.VMEM((steps, rows, width), jnp.float32),
            pltpu.VMEM((rows, 128), jnp.float32),
            pltpu.VMEM((steps, nz - 1, 2 * block, width // 2), jnp.bfloat16),
            pltpu.VMEM((steps, nz - 1, 2 * block, width // 2), jnp.bfloat16),
            pltpu.VMEM((nz - 1, block, 128), jnp.float32),
            pltpu.VMEM((nz - 1, block, 128), jnp.float32),
            dma((nn - 1,)),
            dma((nn - 1,)),
            dma((steps, 2)),
            dma((steps,)),
            dma((steps,)),
            dma,
            dma,
            dma((steps, nz - 1)),
            dma((steps, nz - 1)),
            dma((nz - 1,)),
            dma((nz - 1,)),
            dma((steps,)),
            dma((steps,)),
        ],
        compiler_params=pltpu.CompilerParams(
            collective_id=0, has_side_effects=True, vmem_limit_bytes=56 << 20
        ),
    )(tokens, norm_gain[None, :], w_query, w_key, w_value)


def project_kernel(
    nz, nn, own_rows, heads_ref, w_ref, out_ref,
    held, lhs, weights, total_ref, parts, recv_parts,
    w_sem, right_s, left_s, right_r, left_r, sib_s, sib_r, x_ss, x_rs,
):
    me = lax.axis_index("wide")
    across = lax.axis_index("narrow")
    z, core = me // 2, lax.rem(me, 2)
    sib_index = me + 1 - 2 * core
    sibling = {"wide": sib_index}
    right, left = {"wide": me + 2}, {"wide": me - 2}
    has_right, has_left = z < nz - 1, z > 0
    n_wide = 2 * nz
    tiles = w_ref.shape[1] // TILE
    piece = w_ref.shape[0] // (PARTS * CHUNKS)
    out_rows = out_ref.shape[0]

    def fetch(s, q):
        span = pl.ds((q * CHUNKS + s) * piece, piece)
        return pltpu.make_async_copy(w_ref.at[span, :], weights.at[s, q], w_sem.at[s, q])

    for s in range(CHUNKS):
        for q in range(PARTS):
            fetch(s, q).start()

    barrier = pltpu.get_barrier_semaphore()

    def greet(device):
        pl.semaphore_signal(barrier, inc=1, device_id=device, device_id_type=MESH)

    greet(sibling)
    for d in range(1, nn):
        greet({"narrow": lax.rem(across + d, nn)})

    @pl.when(has_right)
    def _():
        greet(right)

    @pl.when(has_left)
    def _():
        greet(left)

    ends = jnp.where(has_right, 1, 0) + jnp.where(has_left, 1, 0)
    pl.semaphore_wait(barrier, nn + ends)

    def to_right(h, s):
        slot = held.at[me - 2 * h, s]
        return remote(slot, slot, right_s.at[h, s], right_r.at[h, s], right)

    def to_left(h, s):
        slot = held.at[me + 2 * h, s]
        return remote(slot, slot, left_s.at[h, s], left_r.at[h, s], left)

    def to_sibling(k, s, index):
        slot = held.at[index, s]
        return remote(slot, slot, sib_s.at[k, s], sib_r.at[k, s], sibling)

    held[me] = heads_ref[...]

    def send_own(s):
        @pl.when(has_right)
        def _():
            to_right(0, s).start()

        @pl.when(has_left)
        def _():
            to_left(0, s).start()

        to_sibling(0, s, me).start()

    def relay(h, s):
        @pl.when(z - h >= 0)
        def _():
            slot = held.at[me - 2 * h, s]
            remote(slot, slot, right_s.at[h - 1, s], right_r.at[h - 1, s], left).wait_recv()

            @pl.when(has_right)
            def _():
                to_right(h, s).start()

            to_sibling(h, s, me - 2 * h).start()

        @pl.when(z + h < nz)
        def _():
            slot = held.at[me + 2 * h, s]
            remote(slot, slot, left_s.at[h - 1, s], left_r.at[h - 1, s], right).wait_recv()

            @pl.when(has_left)
            def _():
                to_left(h, s).start()

            to_sibling(nz - 1 + h, s, me + 2 * h).start()

    def from_sibling(s):
        to_sibling(0, s, sib_index).wait_recv()
        for h in range(1, nz):

            @pl.when(z - h >= 0)
            def _():
                to_sibling(h, s, sib_index - 2 * h).wait_recv()

            @pl.when(z + h < nz)
            def _():
                to_sibling(nz - 1 + h, s, sib_index + 2 * h).wait_recv()

    def gather_rows(s):
        blocks = [held[b, s].astype(jnp.float32) for b in range(n_wide)]
        for q in range(PARTS):
            rows = [block[q * own_rows : (q + 1) * own_rows] for block in blocks]
            lhs[q] = jnp.concatenate(rows, axis=0).astype(jnp.bfloat16)
            fetch(s, q).wait()

    def exchange(d, t):
        to = lax.rem(across + d, nn)
        cols = pl.ds(pl.multiple_of(t * TILE, TILE), TILE)
        return remote(
            parts.at[to, :, cols],
            recv_parts.at[d - 1, :, cols],
            x_ss.at[d - 1, t],
            x_rs.at[d - 1, t],
            {"narrow": to},
        )

    def product(s, t):
        cols = pl.ds(pl.multiple_of(t * TILE, TILE), TILE)
        acc = None if s == 0 else total_ref[:, cols]
        for q in range(PARTS):
            term = jnp.dot(lhs[q], weights[s, q, :, cols], preferred_element_type=jnp.float32)
            acc = term if acc is None else acc + term
        return acc

    def multiply(s, first, end):
        def body(t, carry):
            cols = pl.ds(pl.multiple_of(t * TILE, TILE), TILE)
            total_ref[:, cols] = product(s, t)
            return carry

        lax.fori_loop(first, end, body, 0)

    send_own(0)
    for h in range(1, nz):
        if h == 1:
            send_own(1)
        relay(h, 0)
    from_sibling(0)
    for s in range(CHUNKS - 1):
        gather_rows(s)
        if s + 2 < CHUNKS:
            send_own(s + 2)
        for h in range(1, nz):
            relay(h, s + 1)
            multiply(s, (h - 1) * tiles // (nz - 1), h * tiles // (nz - 1))
        from_sibling(s + 1)
    gather_rows(CHUNKS - 1)

    def last_multiply(t, carry):
        dense = product(CHUNKS - 1, t).astype(jnp.bfloat16)
        cols = pl.ds(pl.multiple_of(t * TILE, TILE), TILE)
        for p in range(nn):
            parts[p, :, cols] = dense[p * out_rows : (p + 1) * out_rows]
        for d in range(1, nn):
            exchange(d, t).start()
        return carry

    lax.fori_loop(0, tiles, last_multiply, 0)

    def finish(t, carry):
        cols = pl.ds(pl.multiple_of(t * TILE, TILE), TILE)
        total = parts[across, :, cols].astype(jnp.float32)
        for d in range(1, nn):
            exchange(d, t).wait_recv()
            total = total + recv_parts[d - 1, :, cols].astype(jnp.float32)
        out_ref[:, cols] = total.astype(jnp.bfloat16)
        for d in range(1, nn):
            exchange(d, t).wait_send()
        return carry

    lax.fori_loop(0, tiles, finish, 0)

    for s in range(CHUNKS):
        to_sibling(0, s, me).wait_send()
        for h in range(nz):

            @pl.when(jnp.logical_and(z - h >= 0, has_right))
            def _():
                to_right(h, s).wait_send()

            @pl.when(jnp.logical_and(z + h < nz, has_left))
            def _():
                to_left(h, s).wait_send()

            if h > 0:

                @pl.when(z - h >= 0)
                def _():
                    to_sibling(h, s, me - 2 * h).wait_send()

                @pl.when(z + h < nz)
                def _():
                    to_sibling(nz - 1 + h, s, me + 2 * h).wait_send()


def project(heads, w_out, n_wide, nn, own_rows):
    nz = n_wide // 2
    depth, cols = w_out.shape
    piece = depth // (PARTS * CHUNKS)
    tiles = cols // TILE
    out_rows = n_wide * own_rows // nn
    dma = pltpu.SemaphoreType.DMA
    return pl.pallas_call(
        functools.partial(project_kernel, nz, nn, own_rows),
        out_shape=jax.ShapeDtypeStruct((out_rows, cols), jnp.bfloat16),
        in_specs=[
            pl.BlockSpec(memory_space=pltpu.VMEM),
            pl.BlockSpec(memory_space=pl.ANY),
        ],
        out_specs=pl.BlockSpec(memory_space=pltpu.VMEM),
        scratch_shapes=[
            pltpu.VMEM((n_wide, CHUNKS, PARTS * own_rows, piece), jnp.bfloat16),
            pltpu.VMEM((PARTS, n_wide * own_rows, piece), jnp.bfloat16),
            pltpu.VMEM((CHUNKS, PARTS, piece, cols), jnp.bfloat16),
            pltpu.VMEM((n_wide * own_rows, cols), jnp.float32),
            pltpu.VMEM((nn, out_rows, cols), jnp.bfloat16),
            pltpu.VMEM((nn - 1, out_rows, cols), jnp.bfloat16),
            dma((CHUNKS, PARTS)),
            dma((nz, CHUNKS)),
            dma((nz, CHUNKS)),
            dma((nz, CHUNKS)),
            dma((nz, CHUNKS)),
            dma((2 * nz - 1, CHUNKS)),
            dma((2 * nz - 1, CHUNKS)),
            dma((nn - 1, tiles)),
            dma((nn - 1, tiles)),
        ],
        compiler_params=pltpu.CompilerParams(
            collective_id=1, has_side_effects=True, vmem_limit_bytes=56 << 20
        ),
    )(heads, w_out)


def per_device(
    n_wide, nn, tokens, norm_gain, w_query, w_key, w_value, w_out, cache_key, cache_value, lengths
):
    own_rows = cache_key.shape[0]
    index = lax.axis_index("wide")
    row_start = index * own_rows
    query_cols = w_query.shape[1]
    kv_cols = w_key.shape[1]
    chip_sums, chip_squares = project_in(
        tokens, norm_gain, w_query, w_key, w_value, n_wide, nn
    )
    chip_start = lax.rem(index, 2) * own_rows
    mean = lax.dynamic_slice_in_dim(chip_squares, chip_start, own_rows, 0)[:, :1] / D
    own_sums = lax.dynamic_slice_in_dim(chip_sums, chip_start, own_rows, 2)
    last = own_sums.shape[0] - 1
    summed = jnp.concatenate(
        [
            own_sums[:last].transpose(2, 1, 0, 3).reshape(own_rows, query_cols),
            own_sums[last].transpose(1, 0, 2).reshape(own_rows, 2 * kv_cols),
        ],
        axis=1,
    )
    summed = summed * lax.rsqrt(mean + norm_eps)
    own_lengths = lax.dynamic_slice_in_dim(lengths, row_start, own_rows, 0)
    queries = rotate(
        summed[:, :query_cols].reshape(own_rows, query_cols // HD, HD), own_lengths
    ).astype(jnp.bfloat16)
    key_new = rotate(
        summed[:, query_cols : query_cols + kv_cols].reshape(own_rows, kv_cols // HD, HD),
        own_lengths,
    ).astype(jnp.bfloat16)
    value_new = (
        summed[:, query_cols + kv_cols :].reshape(own_rows, kv_cols // HD, HD).astype(jnp.bfloat16)
    )
    heads_out = attend(queries, key_new, value_new, cache_key, cache_value, own_lengths)
    piece = query_cols // (PARTS * CHUNKS)
    stacked = heads_out.reshape(own_rows, PARTS, CHUNKS, piece).transpose(2, 1, 0, 3)
    stacked = stacked.reshape(CHUNKS, PARTS * own_rows, piece)
    return project(stacked, w_out, n_wide, nn, own_rows)


def solution(mesh):
    return jax.shard_map(
        functools.partial(per_device, mesh.shape["wide"], mesh.shape["narrow"]),
        mesh=mesh,
        in_specs=(
            P(("groups", "narrow"), "wide"),
            P("wide"),
            P("wide", "narrow"),
            P("wide", "narrow"),
            P("wide", "narrow"),
            P("narrow", "wide"),
            P(("groups", "wide"), None, "narrow"),
            P(("groups", "wide"), None, "narrow"),
            P("groups"),
        ),
        out_specs=P(("groups", "narrow"), "wide"),
        check_vma=False,
    )
```

```python
import functools

import jax
import jax.numpy as jnp
from jax import lax
from jax.experimental import pallas as pl
from jax.experimental.pallas import tpu as pltpu
from jax.sharding import PartitionSpec as P

D = 16384
HD = 128
PARTS = 4
CHUNKS = 2
TILE = 512
MESH = pl.DeviceIdType.MESH


rope_base = 500000.0
norm_eps = 1e-05


def rotate(vectors, positions):
    half_dim = vectors.shape[-1] // 2
    frequency = rope_base ** (-jnp.arange(half_dim, dtype=jnp.float32) / half_dim)
    angles = positions.astype(jnp.float32)[:, None] * frequency[None, :]
    cosine = jnp.cos(angles)[:, None, :]
    sines = jnp.sin(angles)[:, None, :]
    leading_half = vectors[..., :half_dim]
    trailing_half = vectors[..., half_dim:]
    return jnp.concatenate(
        [
            leading_half * cosine - trailing_half * sines,
            trailing_half * cosine + leading_half * sines,
        ],
        axis=-1,
    )


def attend(queries, key_new, value_new, cache_key, cache_value, lengths):
    batch_rows, head_count, head_dim = queries.shape
    group_count = key_new.shape[1]
    per_group = head_count // group_count
    token_count = cache_key.shape[1]
    grouped = queries.reshape(batch_rows, group_count, per_group, head_dim)
    cached_keys = cache_key.reshape(batch_rows, token_count, group_count, head_dim)
    cached_values = cache_value.reshape(batch_rows, token_count, group_count, head_dim)
    score_scale = head_dim ** (-0.5)
    scores = (
        jnp.einsum("rgqd,rtgd->rgqt", grouped, cached_keys, preferred_element_type=jnp.float32)
        * score_scale
    )
    own_score = (
        jnp.einsum("rgqd,rgd->rgq", grouped, key_new, preferred_element_type=jnp.float32)
        * score_scale
    )
    usable = (jnp.arange(token_count)[None, :] < lengths[:, None])[:, None, None, :]
    highest = jnp.maximum(jnp.max(jnp.where(usable, scores, -1e30), axis=-1), own_score)
    weights = jnp.where(usable, jnp.exp(scores - highest[..., None]), 0.0)
    own_weight = jnp.exp(own_score - highest)
    denominator = jnp.sum(weights, axis=-1) + own_weight
    blended = jnp.einsum(
        "rgqt,rtgd->rgqd",
        weights.astype(jnp.bfloat16),
        cached_values,
        preferred_element_type=jnp.float32,
    )
    blended = blended + own_weight[..., None] * value_new.astype(jnp.float32)[:, :, None, :]
    return (
        (blended / denominator[..., None])
        .astype(jnp.bfloat16)
        .reshape(batch_rows, head_count * head_dim)
    )


def remote(src, dst, send_sem, recv_sem, device):
    return pltpu.make_async_remote_copy(
        src_ref=src,
        dst_ref=dst,
        send_sem=send_sem,
        recv_sem=recv_sem,
        device_id=device,
        device_id_type=MESH,
    )


def sums_kernel(
    nz, nn, steps, tok_ref, gain_ref, wq_ref, wk_ref, wv_ref, out_ref, sq_out_ref,
    tok, scaled, sq, weights, x, core_recv, core_sq, send_buf, recv_buf, sq_send, sq_recv,
    tok_s, tok_r, w_sem, core_ss, core_rs, csq_s, csq_r, z_ss, z_rs, zsq_ss, zsq_rs, fin_ss, fin_rs,
):
    me = lax.axis_index("wide")
    across = lax.axis_index("narrow")
    z, core = me // 2, lax.rem(me, 2)
    away = 1 - core
    sibling = {"wide": me + 1 - 2 * core}
    part_rows = tok_ref.shape[0]
    rows = part_rows * nn
    width = wk_ref.shape[1]
    block = rows // nz
    peers = [lax.rem(z + d, nz) for d in range(1, nz)]

    def query_weights(t, which):
        start = pl.multiple_of((which * (steps - 1) + t) * width, 128)
        return pltpu.make_async_copy(
            wq_ref.at[:, pl.ds(start, width)], weights.at[t, which], w_sem.at[t, which]
        )

    for t in range(steps - 1):
        query_weights(t, away).start()
        query_weights(t, core).start()
    last = steps - 1
    pltpu.make_async_copy(wk_ref, weights.at[last, 0], w_sem.at[last, 0]).start()
    pltpu.make_async_copy(wv_ref, weights.at[last, 1], w_sem.at[last, 1]).start()

    barrier = pltpu.get_barrier_semaphore()

    def greet(device):
        pl.semaphore_signal(barrier, inc=1, device_id=device, device_id_type=MESH)

    greet(sibling)
    for peer in peers:
        greet({"wide": peer * 2 + core})
    for d in range(1, nn):
        greet({"narrow": lax.rem(across + d, nn)})
    pl.semaphore_wait(barrier, nz + nn - 1)

    tok_copies = []
    for d in range(1, nn):
        copy = remote(
            tok_ref,
            tok.at[d - 1],
            tok_s.at[d - 1],
            tok_r.at[d - 1],
            {"narrow": lax.rem(across + d, nn)},
        )
        copy.start()
        tok_copies.append(copy)

    def take(values, origin):
        features = values.astype(jnp.float32)
        span = pl.ds(pl.multiple_of(origin * part_rows, 16), part_rows)
        total = jnp.sum(features * features, axis=1, keepdims=True)
        sq[span, :] = jnp.broadcast_to(total, (part_rows, 128))
        scaled[span, :] = (features * gain_ref[...]).astype(jnp.bfloat16)

    take(tok_ref[...], across)
    for d in range(1, nn):
        tok_copies[d - 1].wait_recv()
        take(tok[d - 1], lax.rem(across + nn - d, nn))

    csq = remote(sq, core_sq, csq_s, csq_r, sibling)
    csq.start()

    def to_core(t):
        return remote(x.at[t, away], core_recv.at[t], core_ss.at[t], core_rs.at[t], sibling)

    def to_chip(t, d):
        return remote(
            send_buf.at[t, d],
            recv_buf.at[t, d],
            z_ss.at[t, d],
            z_rs.at[t, d],
            {"wide": peers[d] * 2 + core},
        )

    def final(t, which):
        return remote(
            out_ref.at[t, which], out_ref.at[t, which], fin_ss.at[t], fin_rs.at[t], sibling
        )

    def multiply(t, which):
        pltpu.make_async_copy(
            wq_ref.at[:, pl.ds(0, width)], weights.at[t, which], w_sem.at[t, which]
        ).wait()
        x[t, which] = jnp.dot(
            scaled[...], weights[t, which], preferred_element_type=jnp.float32
        )

    def forward(t):
        to_core(t).wait_recv()
        for d, peer in enumerate(peers):
            span = pl.ds(pl.multiple_of(peer * block, 8), block)
            both = x[t, core, span, :] + core_recv[t, span, :]
            send_buf[t, d] = jnp.concatenate(
                [both[:, : width // 2], both[:, width // 2 :]], axis=0
            ).astype(jnp.bfloat16)
            to_chip(t, d).start()

    def step(t, carry):
        multiply(t, away)
        to_core(t).start()
        multiply(t, core)

        @pl.when(t > 0)
        def _():
            forward(t - 1)

        return carry

    lax.fori_loop(0, steps, step, 0)
    forward(steps - 1)

    csq.wait_recv()
    sq_copies = []
    for d, peer in enumerate(peers):
        span = pl.ds(pl.multiple_of(peer * block, 8), block)
        sq_send[d] = sq[span, :] + core_sq[span, :]
        copy = remote(
            sq_send.at[d], sq_recv.at[d], zsq_ss.at[d], zsq_rs.at[d], {"wide": peer * 2 + core}
        )
        copy.start()
        sq_copies.append(copy)
    mine = pl.ds(pl.multiple_of(z * block, 8), block)

    def collect(t, carry):
        acc = x[t, core, mine, :] + core_recv[t, mine, :]
        left, right = acc[:, : width // 2], acc[:, width // 2 :]
        for d in range(nz - 1):
            to_chip(t, d).wait_recv()
            got = recv_buf[t, d].astype(jnp.float32)
            left = left + got[:block]
            right = right + got[block:]
        out_ref[t, core] = jnp.concatenate([left, right], axis=1)
        final(t, core).start()
        return carry

    lax.fori_loop(0, steps, collect, 0)
    total = sq[mine, :] + core_sq[mine, :]
    for d in range(nz - 1):
        sq_copies[d].wait_recv()
        total = total + sq_recv[d]
    sq_out_ref[...] = total

    def drain(t, carry):
        to_core(t).wait_send()
        for d in range(nz - 1):
            to_chip(t, d).wait_send()
        final(t, core).wait_send()
        final(t, away).wait_recv()
        return carry

    lax.fori_loop(0, steps, drain, 0)
    csq.wait_send()
    for copy in tok_copies + sq_copies:
        copy.wait_send()


def project_in(tokens, norm_gain, w_query, w_key, w_value, n_wide, nn):
    nz = n_wide // 2
    part_rows, depth = tokens.shape
    rows = part_rows * nn
    block = rows // nz
    width = w_key.shape[1]
    steps = w_query.shape[1] // (2 * width) + 1
    vmem = pl.BlockSpec(memory_space=pltpu.VMEM)
    hbm = pl.BlockSpec(memory_space=pl.ANY)
    dma = pltpu.SemaphoreType.DMA
    return pl.pallas_call(
        functools.partial(sums_kernel, nz, nn, steps),
        out_shape=(
            jax.ShapeDtypeStruct((steps, 2, block, width), jnp.float32),
            jax.ShapeDtypeStruct((block, 128), jnp.float32),
        ),
        in_specs=[vmem, vmem, hbm, hbm, hbm],
        out_specs=(vmem, vmem),
        scratch_shapes=[
            pltpu.VMEM((nn - 1, part_rows, depth), jnp.bfloat16),
            pltpu.VMEM((rows, depth), jnp.bfloat16),
            pltpu.VMEM((rows, 128), jnp.float32),
            pltpu.VMEM((steps, 2, depth, width), jnp.bfloat16),
            pltpu.VMEM((steps, 2, rows, width), jnp.float32),
            pltpu.VMEM((steps, rows, width), jnp.float32),
            pltpu.VMEM((rows, 128), jnp.float32),
            pltpu.VMEM((steps, nz - 1, 2 * block, width // 2), jnp.bfloat16),
            pltpu.VMEM((steps, nz - 1, 2 * block, width // 2), jnp.bfloat16),
            pltpu.VMEM((nz - 1, block, 128), jnp.float32),
            pltpu.VMEM((nz - 1, block, 128), jnp.float32),
            dma((nn - 1,)),
            dma((nn - 1,)),
            dma((steps, 2)),
            dma((steps,)),
            dma((steps,)),
            dma,
            dma,
            dma((steps, nz - 1)),
            dma((steps, nz - 1)),
            dma((nz - 1,)),
            dma((nz - 1,)),
            dma((steps,)),
            dma((steps,)),
        ],
        compiler_params=pltpu.CompilerParams(
            collective_id=0, has_side_effects=True, vmem_limit_bytes=56 << 20
        ),
    )(tokens, norm_gain.astype(jnp.float32)[None, :], w_query, w_key, w_value)


def project_kernel(
    nz, nn, own_rows, heads_ref, w_ref, out_ref,
    held, lhs, weights, total_ref, parts, recv_parts,
    w_sem, right_s, left_s, right_r, left_r, sib_s, sib_r, x_ss, x_rs,
):
    me = lax.axis_index("wide")
    across = lax.axis_index("narrow")
    z, core = me // 2, lax.rem(me, 2)
    sib_index = me + 1 - 2 * core
    sibling = {"wide": sib_index}
    right, left = {"wide": me + 2}, {"wide": me - 2}
    has_right, has_left = z < nz - 1, z > 0
    n_wide = 2 * nz
    tiles = w_ref.shape[1] // TILE
    piece = w_ref.shape[0] // (PARTS * CHUNKS)
    out_rows = out_ref.shape[0]

    def fetch(s, q):
        span = pl.ds((q * CHUNKS + s) * piece, piece)
        return pltpu.make_async_copy(w_ref.at[span, :], weights.at[s, q], w_sem.at[s, q])

    for s in range(CHUNKS):
        for q in range(PARTS):
            fetch(s, q).start()

    barrier = pltpu.get_barrier_semaphore()

    def greet(device):
        pl.semaphore_signal(barrier, inc=1, device_id=device, device_id_type=MESH)

    greet(sibling)
    for d in range(1, nn):
        greet({"narrow": lax.rem(across + d, nn)})

    @pl.when(has_right)
    def _():
        greet(right)

    @pl.when(has_left)
    def _():
        greet(left)

    ends = jnp.where(has_right, 1, 0) + jnp.where(has_left, 1, 0)
    pl.semaphore_wait(barrier, nn + ends)

    def to_right(h, s):
        slot = held.at[me - 2 * h, s]
        return remote(slot, slot, right_s.at[h, s], right_r.at[h, s], right)

    def to_left(h, s):
        slot = held.at[me + 2 * h, s]
        return remote(slot, slot, left_s.at[h, s], left_r.at[h, s], left)

    def to_sibling(k, s, index):
        slot = held.at[index, s]
        return remote(slot, slot, sib_s.at[k, s], sib_r.at[k, s], sibling)

    held[me] = heads_ref[...]

    def send_own(s):
        @pl.when(has_right)
        def _():
            to_right(0, s).start()

        @pl.when(has_left)
        def _():
            to_left(0, s).start()

        to_sibling(0, s, me).start()

    def relay(h, s):
        @pl.when(z - h >= 0)
        def _():
            slot = held.at[me - 2 * h, s]
            remote(slot, slot, right_s.at[h - 1, s], right_r.at[h - 1, s], left).wait_recv()

            @pl.when(has_right)
            def _():
                to_right(h, s).start()

            to_sibling(h, s, me - 2 * h).start()

        @pl.when(z + h < nz)
        def _():
            slot = held.at[me + 2 * h, s]
            remote(slot, slot, left_s.at[h - 1, s], left_r.at[h - 1, s], right).wait_recv()

            @pl.when(has_left)
            def _():
                to_left(h, s).start()

            to_sibling(nz - 1 + h, s, me + 2 * h).start()

    def from_sibling(s):
        to_sibling(0, s, sib_index).wait_recv()
        for h in range(1, nz):

            @pl.when(z - h >= 0)
            def _():
                to_sibling(h, s, sib_index - 2 * h).wait_recv()

            @pl.when(z + h < nz)
            def _():
                to_sibling(nz - 1 + h, s, sib_index + 2 * h).wait_recv()

    def gather_rows(s):
        blocks = [held[b, s].astype(jnp.float32) for b in range(n_wide)]
        for q in range(PARTS):
            rows = [block[q * own_rows : (q + 1) * own_rows] for block in blocks]
            lhs[q] = jnp.concatenate(rows, axis=0).astype(jnp.bfloat16)
            fetch(s, q).wait()

    def exchange(d, t):
        to = lax.rem(across + d, nn)
        cols = pl.ds(pl.multiple_of(t * TILE, TILE), TILE)
        return remote(
            parts.at[to, :, cols],
            recv_parts.at[d - 1, :, cols],
            x_ss.at[d - 1, t],
            x_rs.at[d - 1, t],
            {"narrow": to},
        )

    def product(s, t):
        cols = pl.ds(pl.multiple_of(t * TILE, TILE), TILE)
        acc = None if s == 0 else total_ref[:, cols]
        for q in range(PARTS):
            term = jnp.dot(lhs[q], weights[s, q, :, cols], preferred_element_type=jnp.float32)
            acc = term if acc is None else acc + term
        return acc

    def multiply(s, first, end):
        def body(t, carry):
            cols = pl.ds(pl.multiple_of(t * TILE, TILE), TILE)
            total_ref[:, cols] = product(s, t)
            return carry

        lax.fori_loop(first, end, body, 0)

    send_own(0)
    for h in range(1, nz):
        relay(h, 0)
        if h == 1:
            send_own(1)
    from_sibling(0)
    for s in range(CHUNKS - 1):
        gather_rows(s)
        if s + 2 < CHUNKS:
            send_own(s + 2)
        for h in range(1, nz):
            relay(h, s + 1)
            multiply(s, (h - 1) * tiles // (nz - 1), h * tiles // (nz - 1))
        from_sibling(s + 1)
    gather_rows(CHUNKS - 1)

    def last_multiply(t, carry):
        dense = product(CHUNKS - 1, t).astype(jnp.bfloat16)
        cols = pl.ds(pl.multiple_of(t * TILE, TILE), TILE)
        for p in range(nn):
            parts[p, :, cols] = dense[p * out_rows : (p + 1) * out_rows]
        for d in range(1, nn):
            exchange(d, t).start()
        return carry

    lax.fori_loop(0, tiles, last_multiply, 0)

    def finish(t, carry):
        cols = pl.ds(pl.multiple_of(t * TILE, TILE), TILE)
        total = parts[across, :, cols].astype(jnp.float32)
        for d in range(1, nn):
            exchange(d, t).wait_recv()
            total = total + recv_parts[d - 1, :, cols].astype(jnp.float32)
        out_ref[:, cols] = total.astype(jnp.bfloat16)
        for d in range(1, nn):
            exchange(d, t).wait_send()
        return carry

    lax.fori_loop(0, tiles, finish, 0)

    for s in range(CHUNKS):
        to_sibling(0, s, me).wait_send()
        for h in range(nz):

            @pl.when(jnp.logical_and(z - h >= 0, has_right))
            def _():
                to_right(h, s).wait_send()

            @pl.when(jnp.logical_and(z + h < nz, has_left))
            def _():
                to_left(h, s).wait_send()

            if h > 0:

                @pl.when(z - h >= 0)
                def _():
                    to_sibling(h, s, me - 2 * h).wait_send()

                @pl.when(z + h < nz)
                def _():
                    to_sibling(nz - 1 + h, s, me + 2 * h).wait_send()


def project(heads, w_out, n_wide, nn, own_rows):
    nz = n_wide // 2
    depth, cols = w_out.shape
    piece = depth // (PARTS * CHUNKS)
    tiles = cols // TILE
    out_rows = n_wide * own_rows // nn
    dma = pltpu.SemaphoreType.DMA
    return pl.pallas_call(
        functools.partial(project_kernel, nz, nn, own_rows),
        out_shape=jax.ShapeDtypeStruct((out_rows, cols), jnp.bfloat16),
        in_specs=[
            pl.BlockSpec(memory_space=pltpu.VMEM),
            pl.BlockSpec(memory_space=pl.ANY),
        ],
        out_specs=pl.BlockSpec(memory_space=pltpu.VMEM),
        scratch_shapes=[
            pltpu.VMEM((n_wide, CHUNKS, PARTS * own_rows, piece), jnp.bfloat16),
            pltpu.VMEM((PARTS, n_wide * own_rows, piece), jnp.bfloat16),
            pltpu.VMEM((CHUNKS, PARTS, piece, cols), jnp.bfloat16),
            pltpu.VMEM((n_wide * own_rows, cols), jnp.float32),
            pltpu.VMEM((nn, out_rows, cols), jnp.bfloat16),
            pltpu.VMEM((nn - 1, out_rows, cols), jnp.bfloat16),
            dma((CHUNKS, PARTS)),
            dma((nz, CHUNKS)),
            dma((nz, CHUNKS)),
            dma((nz, CHUNKS)),
            dma((nz, CHUNKS)),
            dma((2 * nz - 1, CHUNKS)),
            dma((2 * nz - 1, CHUNKS)),
            dma((nn - 1, tiles)),
            dma((nn - 1, tiles)),
        ],
        compiler_params=pltpu.CompilerParams(
            collective_id=1, has_side_effects=True, vmem_limit_bytes=56 << 20
        ),
    )(heads, w_out)


def per_device(
    n_wide, nn, tokens, norm_gain, w_query, w_key, w_value, w_out, cache_key, cache_value, lengths
):
    own_rows = cache_key.shape[0]
    index = lax.axis_index("wide")
    row_start = index * own_rows
    query_cols = w_query.shape[1]
    kv_cols = w_key.shape[1]
    chip_sums, chip_squares = project_in(
        tokens, norm_gain, w_query, w_key, w_value, n_wide, nn
    )
    chip_start = lax.rem(index, 2) * own_rows
    mean = lax.dynamic_slice_in_dim(chip_squares, chip_start, own_rows, 0)[:, :1] / D
    own_sums = lax.dynamic_slice_in_dim(chip_sums, chip_start, own_rows, 2)
    last = own_sums.shape[0] - 1
    inverse = lax.rsqrt(mean + norm_eps)[:, :, None]
    own_queries = own_sums[:last].transpose(2, 1, 0, 3).reshape(own_rows, query_cols // HD, HD)
    own_key = own_sums[last, 0].reshape(own_rows, kv_cols // HD, HD)
    own_value = own_sums[last, 1].reshape(own_rows, kv_cols // HD, HD)
    own_lengths = lax.dynamic_slice_in_dim(lengths, row_start, own_rows, 0)
    queries = rotate(own_queries * inverse, own_lengths).astype(jnp.bfloat16)
    key_new = rotate(own_key * inverse, own_lengths).astype(jnp.bfloat16)
    value_new = (own_value * inverse).astype(jnp.bfloat16)
    heads_out = attend(queries, key_new, value_new, cache_key, cache_value, own_lengths)
    piece = query_cols // (PARTS * CHUNKS)
    stacked = heads_out.reshape(own_rows, PARTS, CHUNKS, piece).transpose(2, 1, 0, 3)
    stacked = stacked.reshape(CHUNKS, PARTS * own_rows, piece)
    return project(stacked, w_out, n_wide, nn, own_rows)


def solution(mesh):
    return jax.shard_map(
        functools.partial(per_device, mesh.shape["wide"], mesh.shape["narrow"]),
        mesh=mesh,
        in_specs=(
            P(("groups", "narrow"), "wide"),
            P("wide"),
            P("wide", "narrow"),
            P("wide", "narrow"),
            P("wide", "narrow"),
            P("narrow", "wide"),
            P(("groups", "wide"), None, "narrow"),
            P(("groups", "wide"), None, "narrow"),
            P("groups"),
        ),
        out_specs=P(("groups", "narrow"), "wide"),
        check_vma=False,
    )
```

```python
import functools

import jax
import jax.numpy as jnp
from jax import lax
from jax.experimental import pallas as pl
from jax.experimental.pallas import tpu as pltpu
from jax.sharding import PartitionSpec as P

D = 16384
HD = 128
PARTS = 4
CHUNKS = 2
TILE = 512
MESH = pl.DeviceIdType.MESH


rope_base = 500000.0
norm_eps = 1e-05


def rotate(vectors, positions):
    half_dim = vectors.shape[-1] // 2
    frequency = rope_base ** (-jnp.arange(half_dim, dtype=jnp.float32) / half_dim)
    angles = positions.astype(jnp.float32)[:, None] * frequency[None, :]
    cosine = jnp.cos(angles)[:, None, :]
    sines = jnp.sin(angles)[:, None, :]
    leading_half = vectors[..., :half_dim]
    trailing_half = vectors[..., half_dim:]
    return jnp.concatenate(
        [
            leading_half * cosine - trailing_half * sines,
            trailing_half * cosine + leading_half * sines,
        ],
        axis=-1,
    )


def attend(queries, key_new, value_new, cache_key, cache_value, lengths):
    batch_rows, head_count, head_dim = queries.shape
    group_count = key_new.shape[1]
    per_group = head_count // group_count
    token_count = cache_key.shape[1]
    grouped = queries.reshape(batch_rows, group_count, per_group, head_dim)
    cached_keys = cache_key.reshape(batch_rows, token_count, group_count, head_dim)
    cached_values = cache_value.reshape(batch_rows, token_count, group_count, head_dim)
    score_scale = head_dim ** (-0.5)
    scores = (
        jnp.einsum("rgqd,rtgd->rgqt", grouped, cached_keys, preferred_element_type=jnp.float32)
        * score_scale
    )
    own_score = (
        jnp.einsum("rgqd,rgd->rgq", grouped, key_new, preferred_element_type=jnp.float32)
        * score_scale
    )
    usable = (jnp.arange(token_count)[None, :] < lengths[:, None])[:, None, None, :]
    highest = jnp.maximum(jnp.max(jnp.where(usable, scores, -1e30), axis=-1), own_score)
    weights = jnp.where(usable, jnp.exp(scores - highest[..., None]), 0.0)
    own_weight = jnp.exp(own_score - highest)
    denominator = jnp.sum(weights, axis=-1) + own_weight
    blended = jnp.einsum(
        "rgqt,rtgd->rgqd",
        weights.astype(jnp.bfloat16),
        cached_values,
        preferred_element_type=jnp.float32,
    )
    blended = blended + own_weight[..., None] * value_new.astype(jnp.float32)[:, :, None, :]
    return (
        (blended / denominator[..., None])
        .astype(jnp.bfloat16)
        .reshape(batch_rows, head_count * head_dim)
    )


def remote(src, dst, send_sem, recv_sem, device):
    return pltpu.make_async_remote_copy(
        src_ref=src,
        dst_ref=dst,
        send_sem=send_sem,
        recv_sem=recv_sem,
        device_id=device,
        device_id_type=MESH,
    )


def sums_kernel(
    nz, nn, steps, tok_ref, gain_ref, wq_ref, wk_ref, wv_ref, out_ref, sq_out_ref,
    tok, scaled, sq, weights, x, core_recv, core_sq, send_buf, recv_buf, sq_send, sq_recv,
    tok_s, tok_r, w_sem, core_ss, core_rs, csq_s, csq_r, z_ss, z_rs, zsq_ss, zsq_rs, fin_ss, fin_rs,
):
    me = lax.axis_index("wide")
    across = lax.axis_index("narrow")
    z, core = me // 2, lax.rem(me, 2)
    away = 1 - core
    sibling = {"wide": me + 1 - 2 * core}
    part_rows = tok_ref.shape[0]
    rows = part_rows * nn
    width = wk_ref.shape[1]
    block = rows // nz
    peers = [lax.rem(z + d, nz) for d in range(1, nz)]

    def query_weights(t, which):
        start = pl.multiple_of((which * (steps - 1) + t) * width, 128)
        return pltpu.make_async_copy(
            wq_ref.at[:, pl.ds(start, width)], weights.at[t, which], w_sem.at[t, which]
        )

    last = steps - 1
    ahead = min(3, last)

    def fetch_kv():
        pltpu.make_async_copy(wk_ref, weights.at[last, 0], w_sem.at[last, 0]).start()
        pltpu.make_async_copy(wv_ref, weights.at[last, 1], w_sem.at[last, 1]).start()

    for t in range(ahead):
        query_weights(t, away).start()
        query_weights(t, core).start()

    barrier = pltpu.get_barrier_semaphore()

    def greet(device):
        pl.semaphore_signal(barrier, inc=1, device_id=device, device_id_type=MESH)

    greet(sibling)
    for peer in peers:
        greet({"wide": peer * 2 + core})
    for d in range(1, nn):
        greet({"narrow": lax.rem(across + d, nn)})
    pl.semaphore_wait(barrier, nz + nn - 1)

    tok_copies = []
    for d in range(1, nn):
        copy = remote(
            tok_ref,
            tok.at[d - 1],
            tok_s.at[d - 1],
            tok_r.at[d - 1],
            {"narrow": lax.rem(across + d, nn)},
        )
        copy.start()
        tok_copies.append(copy)

    def take(values, origin):
        features = values.astype(jnp.float32)
        span = pl.ds(pl.multiple_of(origin * part_rows, 16), part_rows)
        total = jnp.sum(features * features, axis=1, keepdims=True)
        sq[span, :] = jnp.broadcast_to(total, (part_rows, 128))
        scaled[span, :] = (features * gain_ref[...][None, :]).astype(jnp.bfloat16)

    take(tok_ref[...], across)
    for d in range(1, nn):
        tok_copies[d - 1].wait_recv()
        take(tok[d - 1], lax.rem(across + nn - d, nn))

    csq = remote(sq, core_sq, csq_s, csq_r, sibling)
    csq.start()

    def to_core(t):
        return remote(x.at[t, away], core_recv.at[t], core_ss.at[t], core_rs.at[t], sibling)

    def to_chip(t, d):
        return remote(
            send_buf.at[t, d],
            recv_buf.at[t, d],
            z_ss.at[t, d],
            z_rs.at[t, d],
            {"wide": peers[d] * 2 + core},
        )

    def final(t, which):
        return remote(
            out_ref.at[t, which], out_ref.at[t, which], fin_ss.at[t], fin_rs.at[t], sibling
        )

    def multiply(t, which):
        pltpu.make_async_copy(
            wq_ref.at[:, pl.ds(0, width)], weights.at[t, which], w_sem.at[t, which]
        ).wait()
        x[t, which] = jnp.dot(
            scaled[...], weights[t, which], preferred_element_type=jnp.float32
        )

    def forward(t):
        to_core(t).wait_recv()
        for d, peer in enumerate(peers):
            span = pl.ds(pl.multiple_of(peer * block, 8), block)
            both = x[t, core, span, :] + core_recv[t, span, :]
            send_buf[t, d] = jnp.concatenate(
                [both[:, : width // 2], both[:, width // 2 :]], axis=0
            ).astype(jnp.bfloat16)
            to_chip(t, d).start()

    def step(t, carry):
        @pl.when(t + ahead < last)
        def _():
            query_weights(t + ahead, away).start()
            query_weights(t + ahead, core).start()

        @pl.when(t + ahead == last)
        def _():
            fetch_kv()

        multiply(t, away)
        to_core(t).start()
        multiply(t, core)

        @pl.when(t > 0)
        def _():
            forward(t - 1)

        return carry

    lax.fori_loop(0, steps, step, 0)
    forward(steps - 1)

    csq.wait_recv()
    sq_copies = []
    for d, peer in enumerate(peers):
        span = pl.ds(pl.multiple_of(peer * block, 8), block)
        sq_send[d] = sq[span, :] + core_sq[span, :]
        copy = remote(
            sq_send.at[d], sq_recv.at[d], zsq_ss.at[d], zsq_rs.at[d], {"wide": peer * 2 + core}
        )
        copy.start()
        sq_copies.append(copy)
    mine = pl.ds(pl.multiple_of(z * block, 8), block)

    def collect(t, carry):
        acc = x[t, core, mine, :] + core_recv[t, mine, :]
        left, right = acc[:, : width // 2], acc[:, width // 2 :]
        for d in range(nz - 1):
            to_chip(t, d).wait_recv()
            got = recv_buf[t, d].astype(jnp.float32)
            left = left + got[:block]
            right = right + got[block:]
        out_ref[t, core] = jnp.concatenate([left, right], axis=1)
        final(t, core).start()
        return carry

    lax.fori_loop(0, steps, collect, 0)
    total = sq[mine, :] + core_sq[mine, :]
    for d in range(nz - 1):
        sq_copies[d].wait_recv()
        total = total + sq_recv[d]
    sq_out_ref[...] = total

    def drain(t, carry):
        to_core(t).wait_send()
        for d in range(nz - 1):
            to_chip(t, d).wait_send()
        final(t, core).wait_send()
        final(t, away).wait_recv()
        return carry

    lax.fori_loop(0, steps, drain, 0)
    csq.wait_send()
    for copy in tok_copies + sq_copies:
        copy.wait_send()


def project_in(tokens, norm_gain, w_query, w_key, w_value, n_wide, nn):
    nz = n_wide // 2
    part_rows, depth = tokens.shape
    rows = part_rows * nn
    block = rows // nz
    width = w_key.shape[1]
    steps = w_query.shape[1] // (2 * width) + 1
    vmem = pl.BlockSpec(memory_space=pltpu.VMEM)
    hbm = pl.BlockSpec(memory_space=pl.ANY)
    dma = pltpu.SemaphoreType.DMA
    return pl.pallas_call(
        functools.partial(sums_kernel, nz, nn, steps),
        out_shape=(
            jax.ShapeDtypeStruct((steps, 2, block, width), jnp.float32),
            jax.ShapeDtypeStruct((block, 128), jnp.float32),
        ),
        in_specs=[vmem, vmem, hbm, hbm, hbm],
        out_specs=(vmem, vmem),
        scratch_shapes=[
            pltpu.VMEM((nn - 1, part_rows, depth), jnp.bfloat16),
            pltpu.VMEM((rows, depth), jnp.bfloat16),
            pltpu.VMEM((rows, 128), jnp.float32),
            pltpu.VMEM((steps, 2, depth, width), jnp.bfloat16),
            pltpu.VMEM((steps, 2, rows, width), jnp.float32),
            pltpu.VMEM((steps, rows, width), jnp.float32),
            pltpu.VMEM((rows, 128), jnp.float32),
            pltpu.VMEM((steps, nz - 1, 2 * block, width // 2), jnp.bfloat16),
            pltpu.VMEM((steps, nz - 1, 2 * block, width // 2), jnp.bfloat16),
            pltpu.VMEM((nz - 1, block, 128), jnp.float32),
            pltpu.VMEM((nz - 1, block, 128), jnp.float32),
            dma((nn - 1,)),
            dma((nn - 1,)),
            dma((steps, 2)),
            dma((steps,)),
            dma((steps,)),
            dma,
            dma,
            dma((steps, nz - 1)),
            dma((steps, nz - 1)),
            dma((nz - 1,)),
            dma((nz - 1,)),
            dma((steps,)),
            dma((steps,)),
        ],
        compiler_params=pltpu.CompilerParams(
            collective_id=0, has_side_effects=True, vmem_limit_bytes=56 << 20
        ),
    )(tokens, norm_gain.astype(jnp.float32), w_query, w_key, w_value)


def project_kernel(
    nz, nn, own_rows, heads_ref, w_ref, out_ref,
    held, lhs, weights, total_ref, parts, recv_parts,
    w_sem, right_s, left_s, right_r, left_r, sib_s, sib_r, x_ss, x_rs,
):
    me = lax.axis_index("wide")
    across = lax.axis_index("narrow")
    z, core = me // 2, lax.rem(me, 2)
    sib_index = me + 1 - 2 * core
    sibling = {"wide": sib_index}
    right, left = {"wide": me + 2}, {"wide": me - 2}
    has_right, has_left = z < nz - 1, z > 0
    n_wide = 2 * nz
    tiles = w_ref.shape[1] // TILE
    piece = w_ref.shape[0] // (PARTS * CHUNKS)
    out_rows = out_ref.shape[0]

    def fetch(s, q):
        span = pl.ds((q * CHUNKS + s) * piece, piece)
        return pltpu.make_async_copy(w_ref.at[span, :], weights.at[s, q], w_sem.at[s, q])

    for q in range(PARTS):
        fetch(0, q).start()

    barrier = pltpu.get_barrier_semaphore()

    def greet(device):
        pl.semaphore_signal(barrier, inc=1, device_id=device, device_id_type=MESH)

    greet(sibling)
    for d in range(1, nn):
        greet({"narrow": lax.rem(across + d, nn)})

    @pl.when(has_right)
    def _():
        greet(right)

    @pl.when(has_left)
    def _():
        greet(left)

    ends = jnp.where(has_right, 1, 0) + jnp.where(has_left, 1, 0)
    pl.semaphore_wait(barrier, nn + ends)

    def to_right(h, s):
        slot = held.at[me - 2 * h, s]
        return remote(slot, slot, right_s.at[h, s], right_r.at[h, s], right)

    def to_left(h, s):
        slot = held.at[me + 2 * h, s]
        return remote(slot, slot, left_s.at[h, s], left_r.at[h, s], left)

    def to_sibling(k, s, index):
        slot = held.at[index, s]
        return remote(slot, slot, sib_s.at[k, s], sib_r.at[k, s], sibling)

    held[me] = heads_ref[...]

    def send_own(s):
        @pl.when(has_right)
        def _():
            to_right(0, s).start()

        @pl.when(has_left)
        def _():
            to_left(0, s).start()

        to_sibling(0, s, me).start()

    def relay(h, s):
        @pl.when(z - h >= 0)
        def _():
            slot = held.at[me - 2 * h, s]
            remote(slot, slot, right_s.at[h - 1, s], right_r.at[h - 1, s], left).wait_recv()

            @pl.when(has_right)
            def _():
                to_right(h, s).start()

            to_sibling(h, s, me - 2 * h).start()

        @pl.when(z + h < nz)
        def _():
            slot = held.at[me + 2 * h, s]
            remote(slot, slot, left_s.at[h - 1, s], left_r.at[h - 1, s], right).wait_recv()

            @pl.when(has_left)
            def _():
                to_left(h, s).start()

            to_sibling(nz - 1 + h, s, me + 2 * h).start()

    def from_sibling(s):
        to_sibling(0, s, sib_index).wait_recv()
        for h in range(1, nz):

            @pl.when(z - h >= 0)
            def _():
                to_sibling(h, s, sib_index - 2 * h).wait_recv()

            @pl.when(z + h < nz)
            def _():
                to_sibling(nz - 1 + h, s, sib_index + 2 * h).wait_recv()

    def gather_rows(s):
        blocks = [held[b, s].astype(jnp.float32) for b in range(n_wide)]
        for q in range(PARTS):
            rows = [block[q * own_rows : (q + 1) * own_rows] for block in blocks]
            lhs[q] = jnp.concatenate(rows, axis=0).astype(jnp.bfloat16)
            fetch(s, q).wait()

    def exchange(d, t):
        to = lax.rem(across + d, nn)
        cols = pl.ds(pl.multiple_of(t * TILE, TILE), TILE)
        return remote(
            parts.at[to, :, cols],
            recv_parts.at[d - 1, :, cols],
            x_ss.at[d - 1, t],
            x_rs.at[d - 1, t],
            {"narrow": to},
        )

    def product(s, t):
        cols = pl.ds(pl.multiple_of(t * TILE, TILE), TILE)
        acc = None if s == 0 else total_ref[:, cols]
        for q in range(PARTS):
            term = jnp.dot(lhs[q], weights[s, q, :, cols], preferred_element_type=jnp.float32)
            acc = term if acc is None else acc + term
        return acc

    def multiply(s, first, end):
        def body(t, carry):
            cols = pl.ds(pl.multiple_of(t * TILE, TILE), TILE)
            total_ref[:, cols] = product(s, t)
            return carry

        lax.fori_loop(first, end, body, 0)

    send_own(0)
    for h in range(1, nz):
        relay(h, 0)
        if h == 1:
            send_own(1)
    from_sibling(0)
    for s in range(CHUNKS - 1):
        gather_rows(s)
        for q in range(PARTS):
            fetch(s + 1, q).start()
        if s + 2 < CHUNKS:
            send_own(s + 2)
        for h in range(1, nz):
            relay(h, s + 1)
            multiply(s, (h - 1) * tiles // (nz - 1), h * tiles // (nz - 1))
        from_sibling(s + 1)
    gather_rows(CHUNKS - 1)

    def last_multiply(t, carry):
        dense = product(CHUNKS - 1, t).astype(jnp.bfloat16)
        cols = pl.ds(pl.multiple_of(t * TILE, TILE), TILE)
        for p in range(nn):
            parts[p, :, cols] = dense[p * out_rows : (p + 1) * out_rows]
        for d in range(1, nn):
            exchange(d, t).start()
        return carry

    lax.fori_loop(0, tiles, last_multiply, 0)

    def finish(t, carry):
        cols = pl.ds(pl.multiple_of(t * TILE, TILE), TILE)
        total = parts[across, :, cols].astype(jnp.float32)
        for d in range(1, nn):
            exchange(d, t).wait_recv()
            total = total + recv_parts[d - 1, :, cols].astype(jnp.float32)
        out_ref[:, cols] = total.astype(jnp.bfloat16)
        for d in range(1, nn):
            exchange(d, t).wait_send()
        return carry

    lax.fori_loop(0, tiles, finish, 0)

    for s in range(CHUNKS):
        to_sibling(0, s, me).wait_send()
        for h in range(nz):

            @pl.when(jnp.logical_and(z - h >= 0, has_right))
            def _():
                to_right(h, s).wait_send()

            @pl.when(jnp.logical_and(z + h < nz, has_left))
            def _():
                to_left(h, s).wait_send()

            if h > 0:

                @pl.when(z - h >= 0)
                def _():
                    to_sibling(h, s, me - 2 * h).wait_send()

                @pl.when(z + h < nz)
                def _():
                    to_sibling(nz - 1 + h, s, me + 2 * h).wait_send()


def project(heads, w_out, n_wide, nn, own_rows):
    nz = n_wide // 2
    depth, cols = w_out.shape
    piece = depth // (PARTS * CHUNKS)
    tiles = cols // TILE
    out_rows = n_wide * own_rows // nn
    dma = pltpu.SemaphoreType.DMA
    return pl.pallas_call(
        functools.partial(project_kernel, nz, nn, own_rows),
        out_shape=jax.ShapeDtypeStruct((out_rows, cols), jnp.bfloat16),
        in_specs=[
            pl.BlockSpec(memory_space=pltpu.VMEM),
            pl.BlockSpec(memory_space=pl.ANY),
        ],
        out_specs=pl.BlockSpec(memory_space=pltpu.VMEM),
        scratch_shapes=[
            pltpu.VMEM((n_wide, CHUNKS, PARTS * own_rows, piece), jnp.bfloat16),
            pltpu.VMEM((PARTS, n_wide * own_rows, piece), jnp.bfloat16),
            pltpu.VMEM((CHUNKS, PARTS, piece, cols), jnp.bfloat16),
            pltpu.VMEM((n_wide * own_rows, cols), jnp.float32),
            pltpu.VMEM((nn, out_rows, cols), jnp.bfloat16),
            pltpu.VMEM((nn - 1, out_rows, cols), jnp.bfloat16),
            dma((CHUNKS, PARTS)),
            dma((nz, CHUNKS)),
            dma((nz, CHUNKS)),
            dma((nz, CHUNKS)),
            dma((nz, CHUNKS)),
            dma((2 * nz - 1, CHUNKS)),
            dma((2 * nz - 1, CHUNKS)),
            dma((nn - 1, tiles)),
            dma((nn - 1, tiles)),
        ],
        compiler_params=pltpu.CompilerParams(
            collective_id=1, has_side_effects=True, vmem_limit_bytes=56 << 20
        ),
    )(heads, w_out)


def per_device(
    n_wide, nn, tokens, norm_gain, w_query, w_key, w_value, w_out, cache_key, cache_value, lengths
):
    own_rows = cache_key.shape[0]
    index = lax.axis_index("wide")
    row_start = index * own_rows
    query_cols = w_query.shape[1]
    kv_cols = w_key.shape[1]
    chip_sums, chip_squares = project_in(
        tokens, norm_gain, w_query, w_key, w_value, n_wide, nn
    )
    chip_start = lax.rem(index, 2) * own_rows
    mean = lax.dynamic_slice_in_dim(chip_squares, chip_start, own_rows, 0)[:, :1] / D
    own_sums = lax.dynamic_slice_in_dim(chip_sums, chip_start, own_rows, 2)
    last = own_sums.shape[0] - 1
    inverse = lax.rsqrt(mean + norm_eps)[:, :, None]
    own_queries = own_sums[:last].transpose(2, 1, 0, 3).reshape(own_rows, query_cols // HD, HD)
    own_key = own_sums[last, 0].reshape(own_rows, kv_cols // HD, HD)
    own_value = own_sums[last, 1].reshape(own_rows, kv_cols // HD, HD)
    own_lengths = lax.dynamic_slice_in_dim(lengths, row_start, own_rows, 0)
    queries = rotate(own_queries * inverse, own_lengths).astype(jnp.bfloat16)
    key_new = rotate(own_key * inverse, own_lengths).astype(jnp.bfloat16)
    value_new = (own_value * inverse).astype(jnp.bfloat16)
    heads_out = attend(queries, key_new, value_new, cache_key, cache_value, own_lengths)
    piece = query_cols // (PARTS * CHUNKS)
    stacked = heads_out.reshape(own_rows, PARTS, CHUNKS, piece).transpose(2, 1, 0, 3)
    stacked = stacked.reshape(CHUNKS, PARTS * own_rows, piece)
    return project(stacked, w_out, n_wide, nn, own_rows)


def solution(mesh):
    return jax.shard_map(
        functools.partial(per_device, mesh.shape["wide"], mesh.shape["narrow"]),
        mesh=mesh,
        in_specs=(
            P(("groups", "narrow"), "wide"),
            P("wide"),
            P("wide", "narrow"),
            P("wide", "narrow"),
            P("wide", "narrow"),
            P("narrow", "wide"),
            P(("groups", "wide"), None, "narrow"),
            P(("groups", "wide"), None, "narrow"),
            P("groups"),
        ),
        out_specs=P(("groups", "narrow"), "wide"),
        check_vma=False,
    )
```

```python
import functools

import jax
import jax.numpy as jnp
from jax import lax
from jax.experimental import pallas as pl
from jax.experimental.pallas import tpu as pltpu
from jax.sharding import PartitionSpec as P

D = 16384
HD = 128
PARTS = 4
CHUNKS = 2
TILE = 512
MESH = pl.DeviceIdType.MESH


rope_base = 500000.0
norm_eps = 1e-05


def rotate(vectors, positions):
    half_dim = vectors.shape[-1] // 2
    frequency = rope_base ** (-jnp.arange(half_dim, dtype=jnp.float32) / half_dim)
    angles = positions.astype(jnp.float32)[:, None] * frequency[None, :]
    cosine = jnp.cos(angles)[:, None, :]
    sines = jnp.sin(angles)[:, None, :]
    leading_half = vectors[..., :half_dim]
    trailing_half = vectors[..., half_dim:]
    return jnp.concatenate(
        [
            leading_half * cosine - trailing_half * sines,
            trailing_half * cosine + leading_half * sines,
        ],
        axis=-1,
    )


def attend(queries, key_new, value_new, cache_key, cache_value, lengths):
    batch_rows, head_count, head_dim = queries.shape
    group_count = key_new.shape[1]
    per_group = head_count // group_count
    token_count = cache_key.shape[1]
    grouped = queries.reshape(batch_rows, group_count, per_group, head_dim)
    cached_keys = cache_key.reshape(batch_rows, token_count, group_count, head_dim)
    cached_values = cache_value.reshape(batch_rows, token_count, group_count, head_dim)
    score_scale = head_dim ** (-0.5)
    scores = (
        jnp.einsum("rgqd,rtgd->rgqt", grouped, cached_keys, preferred_element_type=jnp.float32)
        * score_scale
    )
    own_score = (
        jnp.einsum("rgqd,rgd->rgq", grouped, key_new, preferred_element_type=jnp.float32)
        * score_scale
    )
    usable = (jnp.arange(token_count)[None, :] < lengths[:, None])[:, None, None, :]
    highest = jnp.maximum(jnp.max(jnp.where(usable, scores, -1e30), axis=-1), own_score)
    weights = jnp.where(usable, jnp.exp(scores - highest[..., None]), 0.0)
    own_weight = jnp.exp(own_score - highest)
    denominator = jnp.sum(weights, axis=-1) + own_weight
    blended = jnp.einsum(
        "rgqt,rtgd->rgqd",
        weights.astype(jnp.bfloat16),
        cached_values,
        preferred_element_type=jnp.float32,
    )
    blended = blended + own_weight[..., None] * value_new.astype(jnp.float32)[:, :, None, :]
    return (
        (blended / denominator[..., None])
        .astype(jnp.bfloat16)
        .reshape(batch_rows, head_count * head_dim)
    )


def remote(src, dst, send_sem, recv_sem, device):
    return pltpu.make_async_remote_copy(
        src_ref=src,
        dst_ref=dst,
        send_sem=send_sem,
        recv_sem=recv_sem,
        device_id=device,
        device_id_type=MESH,
    )


def sums_kernel(
    nz, nn, steps, tok_ref, gain_ref, wq_ref, wk_ref, wv_ref, out_ref, sq_out_ref,
    tok, scaled, sq, weights, x, core_recv, core_sq, send_buf, recv_buf, sq_send, sq_recv,
    tok_s, tok_r, w_sem, core_ss, core_rs, csq_s, csq_r, z_ss, z_rs, zsq_ss, zsq_rs, fin_ss, fin_rs,
):
    me = lax.axis_index("wide")
    across = lax.axis_index("narrow")
    z, core = me // 2, lax.rem(me, 2)
    away = 1 - core
    sibling = {"wide": me + 1 - 2 * core}
    part_rows = tok_ref.shape[0]
    rows = part_rows * nn
    width = wk_ref.shape[1]
    block = rows // nz
    peers = [lax.rem(z + d, nz) for d in range(1, nz)]

    def query_weights(t, which):
        start = pl.multiple_of((which * (steps - 1) + t) * width, 128)
        return pltpu.make_async_copy(
            wq_ref.at[:, pl.ds(start, width)], weights.at[t, which], w_sem.at[t, which]
        )

    for t in range(steps - 1):
        query_weights(t, away).start()
        query_weights(t, core).start()
    last = steps - 1
    pltpu.make_async_copy(wk_ref, weights.at[last, 0], w_sem.at[last, 0]).start()
    pltpu.make_async_copy(wv_ref, weights.at[last, 1], w_sem.at[last, 1]).start()

    barrier = pltpu.get_barrier_semaphore()

    def greet(device):
        pl.semaphore_signal(barrier, inc=1, device_id=device, device_id_type=MESH)

    greet(sibling)
    for peer in peers:
        greet({"wide": peer * 2 + core})
    for d in range(1, nn):
        greet({"narrow": lax.rem(across + d, nn)})
    pl.semaphore_wait(barrier, nz + nn - 1)

    tok_copies = []
    for d in range(1, nn):
        copy = remote(
            tok_ref,
            tok.at[d - 1],
            tok_s.at[d - 1],
            tok_r.at[d - 1],
            {"narrow": lax.rem(across + d, nn)},
        )
        copy.start()
        tok_copies.append(copy)

    def take(values, origin):
        features = values.astype(jnp.float32)
        span = pl.ds(pl.multiple_of(origin * part_rows, 16), part_rows)
        total = jnp.sum(features * features, axis=1, keepdims=True)
        sq[span, :] = jnp.broadcast_to(total, (part_rows, 128))
        scaled[span, :] = (features * gain_ref[...].astype(jnp.float32)[None, :]).astype(jnp.bfloat16)

    take(tok_ref[...], across)
    for d in range(1, nn):
        tok_copies[d - 1].wait_recv()
        take(tok[d - 1], lax.rem(across + nn - d, nn))

    csq = remote(sq, core_sq, csq_s, csq_r, sibling)
    csq.start()

    def to_core(t):
        return remote(x.at[t, away], core_recv.at[t], core_ss.at[t], core_rs.at[t], sibling)

    def to_chip(t, d):
        return remote(
            send_buf.at[t, d],
            recv_buf.at[t, d],
            z_ss.at[t, d],
            z_rs.at[t, d],
            {"wide": peers[d] * 2 + core},
        )

    def final(t, which):
        return remote(
            out_ref.at[t, which], out_ref.at[t, which], fin_ss.at[t], fin_rs.at[t], sibling
        )

    def multiply(t, which):
        pltpu.make_async_copy(
            wq_ref.at[:, pl.ds(0, width)], weights.at[t, which], w_sem.at[t, which]
        ).wait()
        x[t, which] = jnp.dot(
            scaled[...], weights[t, which], preferred_element_type=jnp.float32
        )

    def forward(t):
        to_core(t).wait_recv()
        for d, peer in enumerate(peers):
            span = pl.ds(pl.multiple_of(peer * block, 8), block)
            both = x[t, core, span, :] + core_recv[t, span, :]
            send_buf[t, d] = jnp.concatenate(
                [both[:, : width // 2], both[:, width // 2 :]], axis=0
            ).astype(jnp.bfloat16)
            to_chip(t, d).start()

    def step(t, carry):
        multiply(t, away)
        to_core(t).start()
        multiply(t, core)

        @pl.when(t > 0)
        def _():
            forward(t - 1)

        return carry

    lax.fori_loop(0, steps, step, 0)
    forward(steps - 1)

    csq.wait_recv()
    sq_copies = []
    for d, peer in enumerate(peers):
        span = pl.ds(pl.multiple_of(peer * block, 8), block)
        sq_send[d] = sq[span, :] + core_sq[span, :]
        copy = remote(
            sq_send.at[d], sq_recv.at[d], zsq_ss.at[d], zsq_rs.at[d], {"wide": peer * 2 + core}
        )
        copy.start()
        sq_copies.append(copy)
    mine = pl.ds(pl.multiple_of(z * block, 8), block)

    def collect(t, carry):
        acc = x[t, core, mine, :] + core_recv[t, mine, :]
        left, right = acc[:, : width // 2], acc[:, width // 2 :]
        for d in range(nz - 1):
            to_chip(t, d).wait_recv()
            got = recv_buf[t, d].astype(jnp.float32)
            left = left + got[:block]
            right = right + got[block:]
        out_ref[t, core] = jnp.concatenate([left, right], axis=1)
        final(t, core).start()
        return carry

    lax.fori_loop(0, steps, collect, 0)
    total = sq[mine, :] + core_sq[mine, :]
    for d in range(nz - 1):
        sq_copies[d].wait_recv()
        total = total + sq_recv[d]
    sq_out_ref[...] = total

    def drain(t, carry):
        to_core(t).wait_send()
        for d in range(nz - 1):
            to_chip(t, d).wait_send()
        final(t, core).wait_send()
        final(t, away).wait_recv()
        return carry

    lax.fori_loop(0, steps, drain, 0)
    csq.wait_send()
    for copy in tok_copies + sq_copies:
        copy.wait_send()


def project_in(tokens, norm_gain, w_query, w_key, w_value, n_wide, nn):
    nz = n_wide // 2
    part_rows, depth = tokens.shape
    rows = part_rows * nn
    block = rows // nz
    width = w_key.shape[1]
    steps = w_query.shape[1] // (2 * width) + 1
    vmem = pl.BlockSpec(memory_space=pltpu.VMEM)
    hbm = pl.BlockSpec(memory_space=pl.ANY)
    dma = pltpu.SemaphoreType.DMA
    return pl.pallas_call(
        functools.partial(sums_kernel, nz, nn, steps),
        out_shape=(
            jax.ShapeDtypeStruct((steps, 2, block, width), jnp.float32),
            jax.ShapeDtypeStruct((block, 128), jnp.float32),
        ),
        in_specs=[vmem, vmem, hbm, hbm, hbm],
        out_specs=(vmem, vmem),
        scratch_shapes=[
            pltpu.VMEM((nn - 1, part_rows, depth), jnp.bfloat16),
            pltpu.VMEM((rows, depth), jnp.bfloat16),
            pltpu.VMEM((rows, 128), jnp.float32),
            pltpu.VMEM((steps, 2, depth, width), jnp.bfloat16),
            pltpu.VMEM((steps, 2, rows, width), jnp.float32),
            pltpu.VMEM((steps, rows, width), jnp.float32),
            pltpu.VMEM((rows, 128), jnp.float32),
            pltpu.VMEM((steps, nz - 1, 2 * block, width // 2), jnp.bfloat16),
            pltpu.VMEM((steps, nz - 1, 2 * block, width // 2), jnp.bfloat16),
            pltpu.VMEM((nz - 1, block, 128), jnp.float32),
            pltpu.VMEM((nz - 1, block, 128), jnp.float32),
            dma((nn - 1,)),
            dma((nn - 1,)),
            dma((steps, 2)),
            dma((steps,)),
            dma((steps,)),
            dma,
            dma,
            dma((steps, nz - 1)),
            dma((steps, nz - 1)),
            dma((nz - 1,)),
            dma((nz - 1,)),
            dma((steps,)),
            dma((steps,)),
        ],
        compiler_params=pltpu.CompilerParams(
            collective_id=0, has_side_effects=True, vmem_limit_bytes=56 << 20
        ),
    )(tokens, norm_gain, w_query, w_key, w_value)


def project_kernel(
    nz, nn, own_rows, heads_ref, w_ref, out_ref,
    held, lhs, weights, total_ref, parts, recv_parts,
    w_sem, right_s, left_s, right_r, left_r, sib_s, sib_r, x_ss, x_rs,
):
    me = lax.axis_index("wide")
    across = lax.axis_index("narrow")
    z, core = me // 2, lax.rem(me, 2)
    sib_index = me + 1 - 2 * core
    sibling = {"wide": sib_index}
    right, left = {"wide": me + 2}, {"wide": me - 2}
    has_right, has_left = z < nz - 1, z > 0
    n_wide = 2 * nz
    tiles = w_ref.shape[1] // TILE
    piece = w_ref.shape[0] // (PARTS * CHUNKS)
    out_rows = out_ref.shape[0]

    def fetch(s, q):
        span = pl.ds((q * CHUNKS + s) * piece, piece)
        return pltpu.make_async_copy(w_ref.at[span, :], weights.at[s, q], w_sem.at[s, q])

    for s in range(CHUNKS):
        for q in range(PARTS):
            fetch(s, q).start()

    barrier = pltpu.get_barrier_semaphore()

    def greet(device):
        pl.semaphore_signal(barrier, inc=1, device_id=device, device_id_type=MESH)

    greet(sibling)
    for d in range(1, nn):
        greet({"narrow": lax.rem(across + d, nn)})

    @pl.when(has_right)
    def _():
        greet(right)

    @pl.when(has_left)
    def _():
        greet(left)

    ends = jnp.where(has_right, 1, 0) + jnp.where(has_left, 1, 0)
    pl.semaphore_wait(barrier, nn + ends)

    def to_right(h, s):
        slot = held.at[me - 2 * h, s]
        return remote(slot, slot, right_s.at[h, s], right_r.at[h, s], right)

    def to_left(h, s):
        slot = held.at[me + 2 * h, s]
        return remote(slot, slot, left_s.at[h, s], left_r.at[h, s], left)

    def to_sibling(k, s, index):
        slot = held.at[index, s]
        return remote(slot, slot, sib_s.at[k, s], sib_r.at[k, s], sibling)

    held[me] = heads_ref[...]

    def send_own(s):
        @pl.when(has_right)
        def _():
            to_right(0, s).start()

        @pl.when(has_left)
        def _():
            to_left(0, s).start()

        to_sibling(0, s, me).start()

    def relay(h, s):
        @pl.when(z - h >= 0)
        def _():
            slot = held.at[me - 2 * h, s]
            remote(slot, slot, right_s.at[h - 1, s], right_r.at[h - 1, s], left).wait_recv()

            @pl.when(has_right)
            def _():
                to_right(h, s).start()

            to_sibling(h, s, me - 2 * h).start()

        @pl.when(z + h < nz)
        def _():
            slot = held.at[me + 2 * h, s]
            remote(slot, slot, left_s.at[h - 1, s], left_r.at[h - 1, s], right).wait_recv()

            @pl.when(has_left)
            def _():
                to_left(h, s).start()

            to_sibling(nz - 1 + h, s, me + 2 * h).start()

    def from_sibling(s):
        to_sibling(0, s, sib_index).wait_recv()
        for h in range(1, nz):

            @pl.when(z - h >= 0)
            def _():
                to_sibling(h, s, sib_index - 2 * h).wait_recv()

            @pl.when(z + h < nz)
            def _():
                to_sibling(nz - 1 + h, s, sib_index + 2 * h).wait_recv()

    def gather_rows(s):
        blocks = [held[b, s].astype(jnp.float32) for b in range(n_wide)]
        for q in range(PARTS):
            rows = [block[q * own_rows : (q + 1) * own_rows] for block in blocks]
            lhs[q] = jnp.concatenate(rows, axis=0).astype(jnp.bfloat16)
            fetch(s, q).wait()

    def exchange(d, t):
        to = lax.rem(across + d, nn)
        cols = pl.ds(pl.multiple_of(t * TILE, TILE), TILE)
        return remote(
            parts.at[to, :, cols],
            recv_parts.at[d - 1, :, cols],
            x_ss.at[d - 1, t],
            x_rs.at[d - 1, t],
            {"narrow": to},
        )

    def product(s, t):
        cols = pl.ds(pl.multiple_of(t * TILE, TILE), TILE)
        acc = None if s == 0 else total_ref[:, cols]
        for q in range(PARTS):
            term = jnp.dot(lhs[q], weights[s, q, :, cols], preferred_element_type=jnp.float32)
            acc = term if acc is None else acc + term
        return acc

    def multiply(s, first, end):
        def body(t, carry):
            cols = pl.ds(pl.multiple_of(t * TILE, TILE), TILE)
            total_ref[:, cols] = product(s, t)
            return carry

        lax.fori_loop(first, end, body, 0)

    send_own(0)
    for h in range(1, nz):
        relay(h, 0)
        if h == 1:
            send_own(1)
    from_sibling(0)
    for s in range(CHUNKS - 1):
        gather_rows(s)
        if s + 2 < CHUNKS:
            send_own(s + 2)
        for h in range(1, nz):
            relay(h, s + 1)
            multiply(s, (h - 1) * tiles // (nz - 1), h * tiles // (nz - 1))
        from_sibling(s + 1)
    gather_rows(CHUNKS - 1)

    def last_multiply(t, carry):
        dense = product(CHUNKS - 1, t).astype(jnp.bfloat16)
        cols = pl.ds(pl.multiple_of(t * TILE, TILE), TILE)
        for p in range(nn):
            parts[p, :, cols] = dense[p * out_rows : (p + 1) * out_rows]
        for d in range(1, nn):
            exchange(d, t).start()
        return carry

    lax.fori_loop(0, tiles, last_multiply, 0)

    def finish(t, carry):
        cols = pl.ds(pl.multiple_of(t * TILE, TILE), TILE)
        total = parts[across, :, cols].astype(jnp.float32)
        for d in range(1, nn):
            exchange(d, t).wait_recv()
            total = total + recv_parts[d - 1, :, cols].astype(jnp.float32)
        out_ref[:, cols] = total.astype(jnp.bfloat16)
        for d in range(1, nn):
            exchange(d, t).wait_send()
        return carry

    lax.fori_loop(0, tiles, finish, 0)

    for s in range(CHUNKS):
        to_sibling(0, s, me).wait_send()
        for h in range(nz):

            @pl.when(jnp.logical_and(z - h >= 0, has_right))
            def _():
                to_right(h, s).wait_send()

            @pl.when(jnp.logical_and(z + h < nz, has_left))
            def _():
                to_left(h, s).wait_send()

            if h > 0:

                @pl.when(z - h >= 0)
                def _():
                    to_sibling(h, s, me - 2 * h).wait_send()

                @pl.when(z + h < nz)
                def _():
                    to_sibling(nz - 1 + h, s, me + 2 * h).wait_send()


def project(heads, w_out, n_wide, nn, own_rows):
    nz = n_wide // 2
    depth, cols = w_out.shape
    piece = depth // (PARTS * CHUNKS)
    tiles = cols // TILE
    out_rows = n_wide * own_rows // nn
    dma = pltpu.SemaphoreType.DMA
    return pl.pallas_call(
        functools.partial(project_kernel, nz, nn, own_rows),
        out_shape=jax.ShapeDtypeStruct((out_rows, cols), jnp.bfloat16),
        in_specs=[
            pl.BlockSpec(memory_space=pltpu.VMEM),
            pl.BlockSpec(memory_space=pl.ANY),
        ],
        out_specs=pl.BlockSpec(memory_space=pltpu.VMEM),
        scratch_shapes=[
            pltpu.VMEM((n_wide, CHUNKS, PARTS * own_rows, piece), jnp.bfloat16),
            pltpu.VMEM((PARTS, n_wide * own_rows, piece), jnp.bfloat16),
            pltpu.VMEM((CHUNKS, PARTS, piece, cols), jnp.bfloat16),
            pltpu.VMEM((n_wide * own_rows, cols), jnp.float32),
            pltpu.VMEM((nn, out_rows, cols), jnp.bfloat16),
            pltpu.VMEM((nn - 1, out_rows, cols), jnp.bfloat16),
            dma((CHUNKS, PARTS)),
            dma((nz, CHUNKS)),
            dma((nz, CHUNKS)),
            dma((nz, CHUNKS)),
            dma((nz, CHUNKS)),
            dma((2 * nz - 1, CHUNKS)),
            dma((2 * nz - 1, CHUNKS)),
            dma((nn - 1, tiles)),
            dma((nn - 1, tiles)),
        ],
        compiler_params=pltpu.CompilerParams(
            collective_id=1, has_side_effects=True, vmem_limit_bytes=56 << 20
        ),
    )(heads, w_out)


def per_device(
    n_wide, nn, tokens, norm_gain, w_query, w_key, w_value, w_out, cache_key, cache_value, lengths
):
    own_rows = cache_key.shape[0]
    index = lax.axis_index("wide")
    row_start = index * own_rows
    query_cols = w_query.shape[1]
    kv_cols = w_key.shape[1]
    chip_sums, chip_squares = project_in(
        tokens, norm_gain, w_query, w_key, w_value, n_wide, nn
    )
    chip_start = lax.rem(index, 2) * own_rows
    mean = lax.dynamic_slice_in_dim(chip_squares, chip_start, own_rows, 0)[:, :1] / D
    own_sums = lax.dynamic_slice_in_dim(chip_sums, chip_start, own_rows, 2)
    last = own_sums.shape[0] - 1
    inverse = lax.rsqrt(mean + norm_eps)[:, :, None]
    own_queries = own_sums[:last].transpose(2, 1, 0, 3).reshape(own_rows, query_cols // HD, HD)
    own_key = own_sums[last, 0].reshape(own_rows, kv_cols // HD, HD)
    own_value = own_sums[last, 1].reshape(own_rows, kv_cols // HD, HD)
    own_lengths = lax.dynamic_slice_in_dim(lengths, row_start, own_rows, 0)
    queries = rotate(own_queries * inverse, own_lengths).astype(jnp.bfloat16)
    key_new = rotate(own_key * inverse, own_lengths).astype(jnp.bfloat16)
    value_new = (own_value * inverse).astype(jnp.bfloat16)
    heads_out = attend(queries, key_new, value_new, cache_key, cache_value, own_lengths)
    piece = query_cols // (PARTS * CHUNKS)
    stacked = heads_out.reshape(own_rows, PARTS, CHUNKS, piece).transpose(2, 1, 0, 3)
    stacked = stacked.reshape(CHUNKS, PARTS * own_rows, piece)
    return project(stacked, w_out, n_wide, nn, own_rows)


def solution(mesh):
    return jax.shard_map(
        functools.partial(per_device, mesh.shape["wide"], mesh.shape["narrow"]),
        mesh=mesh,
        in_specs=(
            P(("groups", "narrow"), "wide"),
            P("wide"),
            P("wide", "narrow"),
            P("wide", "narrow"),
            P("wide", "narrow"),
            P("narrow", "wide"),
            P(("groups", "wide"), None, "narrow"),
            P(("groups", "wide"), None, "narrow"),
            P("groups"),
        ),
        out_specs=P(("groups", "narrow"), "wide"),
        check_vma=False,
    )
```
